256 devices in a mesh: req: 8 (over x, y_lo), sp: 32 (over y_hi, z, core).
Axes of the slice: x: 4, y: 4 (y_hi: 2, y_lo: 2; y = y_hi * 2 + y_lo), z: 8, core: 2. Of those that a mesh axis runs over, the one named last changes fastest.
Arguments:
- hidden_feats: bfloat16 [65536, 5120], P('req', 'sp'), parts along dimension 0, may hold values from -6 to 6
- mod_shift: float32 [40960], P(('req', 'sp')), parts along dimension 0, may hold values from -3 to 3
- mod_scale: float32 [40960], P(('req', 'sp')), parts along dimension 0, may hold values from -3 to 3
- head_w: bfloat16 [5120, 64], P('sp'), may hold values from -0.078125 to 0.078125
- head_b: float32 [64], replicated, may hold values from -3 to 3
- latent_mean: float32 [16], replicated, may hold values from -3 to 3
- latent_std: float32 [16], replicated, may hold values from 0.5 to 3
- conv_in_w: bfloat16 [3, 3, 3, 16, 384], replicated, may hold values from -0.3125 to 0.3125
- conv_in_b: float32 [384], replicated, may hold values from -3 to 3
- up_w: bfloat16 [3, 3, 384, 192], replicated, may hold values from -0.109375 to 0.109375
- up_b: float32 [192], replicated, may hold values from -3 to 3
Outputs:
- decoded: bfloat16 [64, 64, 256, 192], P('req', None, 'sp'), parts along dimension 0
The draws below stay inside these ranges and needn't reach their ends.
There are 8 independent parts, one for each index of `req`. The reference program is written for one: setup_inputs(seed, part) draws one part's arguments, and reference() takes and returns one part's arrays. A program takes and returns all parts, laid end to end along the dimension named above; an argument that names none is the same for every part. Nothing has to cross between parts.
All inputs are finite; a program needn't handle non-finite values.
Results may differ from the reference program's by a relative error of at most 0.0062.
Values may be sent and summed in bfloat16 or wider, within the bound.
A program may use at most 64 MiB of HBM per device.

```python
import math
import jax
import jax.numpy as jnp
from jax import lax

D = 5120
LAT = 16
CH = 384
CH_UP = 192
PATCH = 64
FR = 8
HP = 16
WP = 64
TOKENS = 8192


def level_of(own_key, dims, pieces, least, top_value):
    level, own = 1.0, jax.random.fold_in(own_key, 6)
    for axis_at, blocks in pieces:
        heights = jnp.exp(jax.random.uniform(jax.random.fold_in(own, axis_at), (blocks,), jnp.float32, least / len(pieces), top_value / len(pieces)))
        level = level * jnp.repeat(heights, dims[axis_at] // blocks).reshape([-1 if axis == axis_at else 1 for axis in range(len(dims))])
    return level


def normal_values(stream_key, shape, deviation, most, cuts=(), held_as=jnp.bfloat16):
    values = deviation * jax.random.normal(stream_key, shape, jnp.float32)
    if cuts:
        values = values * level_of(stream_key, shape, cuts, -0.22, 0.18)
    return jnp.clip(values, -most, most).astype(held_as)


def setup_inputs(seed: int = 0, part: int = 0) -> dict:
    keys = jax.random.split(jax.random.key(seed), 12)
    part_keys = jax.random.split(jax.random.fold_in(keys[11], part), 12)
    return {
        "hidden_feats": normal_values(part_keys[0], (TOKENS, D), 1.0, 6.0, ((1, 32),)),
        "mod_shift": normal_values(part_keys[1], (D,), 0.5, 3.0, ((0, 32),), jnp.float32),
        "mod_scale": normal_values(part_keys[2], (D,), 0.5, 3.0, ((0, 32),), jnp.float32),
        "head_w": normal_values(keys[3], (D, PATCH), D ** -0.5, 0.078125, ((0, 32),)),
        "head_b": normal_values(keys[4], (PATCH,), 0.5, 3.0, (), jnp.float32),
        "latent_mean": normal_values(keys[5], (LAT,), 0.5, 3.0, (), jnp.float32),
        "latent_std": jnp.clip(jnp.exp(jax.random.uniform(keys[6], (LAT,), jnp.float32, math.log(0.5), math.log(3.0))), 0.5, 3.0),
        "conv_in_w": normal_values(keys[7], (3, 3, 3, LAT, CH), (27 * LAT) ** -0.5, 0.3125),
        "conv_in_b": normal_values(keys[8], (CH,), 0.5, 3.0, (), jnp.float32),
        "up_w": normal_values(keys[9], (3, 3, CH, CH_UP), (9 * CH) ** -0.5, 0.109375),
        "up_b": normal_values(keys[10], (CH_UP,), 0.5, 3.0, (), jnp.float32),
    }


def reference(hidden_feats, mod_shift, mod_scale, head_w, head_b, latent_mean, latent_std, conv_in_w, conv_in_b, up_w, up_b):
    feats = hidden_feats.astype(jnp.float32)
    mean = lax.optimization_barrier(jnp.sum(feats, axis=1)) / D
    var = lax.optimization_barrier(jnp.sum(feats * feats, axis=1)) / D - mean * mean
    normed = ((feats - mean[:, None]) * lax.rsqrt(var + 1e-06)[:, None] * (1.0 + mod_scale) + mod_shift).astype(jnp.bfloat16)
    patches = jnp.dot(normed, head_w, preferred_element_type=jnp.float32) + head_b
    grid = patches.reshape(FR, HP, WP, 2, 2, LAT).transpose(0, 1, 3, 2, 4, 5).reshape(FR, 2 * HP, 2 * WP, LAT)
    latent = (grid * latent_std + latent_mean).astype(jnp.bfloat16)
    padded = jnp.pad(latent, ((2, 0), (1, 1), (1, 1), (0, 0)))
    conved = lax.conv_general_dilated(padded[None], conv_in_w, (1, 1, 1), 'VALID', dimension_numbers=('NDHWC', 'DHWIO', 'NDHWC'), preferred_element_type=jnp.float32)[0]
    hidden = (conved + conv_in_b).astype(jnp.bfloat16)
    upsampled = jnp.repeat(jnp.repeat(hidden, 2, axis=1), 2, axis=2)
    upconv = lax.conv_general_dilated(upsampled, up_w, (1, 1), ((1, 1), (1, 1)), dimension_numbers=('NHWC', 'HWIO', 'NHWC'), preferred_element_type=jnp.float32)
    return (upconv + up_b).astype(jnp.bfloat16)
```

```python
import functools

import jax
import jax.numpy as jnp
from jax import lax
from jax.experimental import pallas as pl
from jax.experimental.pallas import tpu as pltpu
from jax.sharding import PartitionSpec as P

F32 = jnp.float32
BF16 = jnp.bfloat16
MESH = pl.DeviceIdType.MESH

FEATS = 5120
LOCAL = 160
FRAMES = 8
CHIPS = 16
GROUP = 32
OFFSETS = [(dy, dz) for dz in (4, 3, 5, 2, 6, 1, 7) for dy in (1, 0)] + [(1, 0), (0, 0)]


def lanes(shape):
    return lax.broadcasted_iota(jnp.int32, shape, len(shape) - 1)


def rows(shape):
    return lax.broadcasted_iota(jnp.int32, shape, len(shape) - 2)


def to_column(row):
    width = row.shape[1]
    square = (width, width)
    return jnp.sum(jnp.where(rows(square) == lanes(square), row, 0.0), axis=1, keepdims=True)


def tile16(row):
    wide = jnp.concatenate([row, jnp.zeros((1, 112), F32)], axis=1)
    for step in (16, 32, 64):
        wide = wide + pltpu.roll(wide, step, 1)
    return wide


def head_kernel(
    x_hbm, shift_ref, scale_ref, head_w_ref, head_b_ref, lat_mean_ref, lat_std_ref,
    out_ref,
    x_buf, partial, sums, squares, own_stat, peer_stat, give, got, kept, parcel, arrived,
    stat_out, stat_in, strip,
    x_sem, stat_sem, core_send, core_recv, send_sem, recv_sem, ssend_sem, srecv_sem, halo_sem,
):
    me = lax.axis_index("sp")
    req = lax.axis_index("req")
    core = lax.rem(me, 2)
    chip = me // 2
    y, z = chip // 8, lax.rem(chip, 8)

    def chip_at(offset):
        dy, dz = offset
        return lax.rem(y + dy, 2) * 8 + lax.rem(z + dz, 8)

    def device(sp):
        return (req, sp)

    partner = chip * 2 + (1 - core)
    left, right = lax.rem(me + GROUP - 1, GROUP), lax.rem(me + 1, GROUP)
    other = jnp.where(core == 0, left, right)

    x_copies = []
    for f in range(FRAMES):
        copy = pltpu.make_async_copy(x_hbm.at[pl.ds(f * 1024, 1024)], x_buf.at[f], x_sem.at[f])
        copy.start()
        x_copies.append(copy)

    barrier = pltpu.get_barrier_semaphore()
    for offset in OFFSETS[:-1]:
        pl.semaphore_signal(barrier, inc=1, device_id=device(chip_at(offset) * 2 + core), device_id_type=MESH)
    pl.semaphore_signal(barrier, inc=1, device_id=device(partner), device_id_type=MESH)
    pl.semaphore_signal(barrier, inc=1, device_id=device(other), device_id_type=MESH)

    scale = to_column(scale_ref[...].reshape(1, LOCAL))
    shift = to_column(shift_ref[...].reshape(1, LOCAL))
    head = head_w_ref[...].astype(F32)
    folded = (1.0 + scale) * head
    column_sum = jnp.sum(folded, axis=0, keepdims=True)
    shifted = jnp.sum(shift * head, axis=0, keepdims=True)
    centred = folded - column_sum * (1.0 / LOCAL)
    high = centred.astype(BF16)
    low = (centred - high.astype(F32)).astype(BF16)
    high = jnp.concatenate([high, high], axis=1)
    low = jnp.concatenate([low, low], axis=1)
    ones = jnp.ones((8, LOCAL), BF16)
    diagonal = rows((128, 128)) == lanes((128, 128))

    for f in range(FRAMES):
        x_copies[f].wait()

        def block(i, carry):
            x = x_buf[f, pl.ds(pl.multiple_of(i * 128, 128), 128), :]
            value = jnp.dot(x, high, preferred_element_type=F32) + jnp.dot(x, low, preferred_element_type=F32)
            partial[pl.ds(pl.multiple_of(f * 1024 + i * 128, 128), 128), :] = value
            transposed = (((1,), (1,)), ((), ()))
            total = lax.dot_general(ones, x, transposed, preferred_element_type=F32)
            gram = lax.dot_general(x, x, transposed, preferred_element_type=F32)
            sums[pl.ds(f * 8 + i, 1), :] = total[0:1, :]
            squares[pl.ds(f * 8 + i, 1), :] = jnp.sum(jnp.where(diagonal, gram, 0.0), axis=0, keepdims=True)
            return carry

        lax.fori_loop(0, 8, block, 0, unroll=True)

    lower = lanes((64, 128)) < 64
    turned = jnp.transpose(jnp.concatenate([sums[...], squares[...]], axis=0))
    top, bottom = turned[0:64], turned[64:128]
    own_stat[0:64, :] = jnp.where(lower, top, pltpu.roll(bottom, 64, 1))
    own_stat[64:128, :] = jnp.where(lower, pltpu.roll(top, 64, 1), bottom)
    own_row = jnp.concatenate([column_sum, shifted], axis=1)
    own_stat[128:136, :] = jnp.broadcast_to(own_row, (8, 128))

    pl.semaphore_wait(barrier, 17)

    stat_copy = pltpu.make_async_remote_copy(
        src_ref=own_stat, dst_ref=peer_stat, send_sem=stat_sem.at[0], recv_sem=stat_sem.at[1],
        device_id=device(partner), device_id_type=MESH,
    )
    stat_copy.start()

    def gathered(chip_to, core_to):
        parts = []
        for parity in range(2):
            at = parity * 64 + (chip_to * 2 + core_to) * 2
            even = partial[pl.ds(at, 64, stride=128), :]
            odd = partial[pl.ds(at + 1, 64, stride=128), :]
            parts.append(jnp.where(lower, even, odd))
        return jnp.concatenate(parts, axis=0)

    core_copies = []
    for k, offset in enumerate(OFFSETS):
        give[k] = gathered(chip_at(offset), 1 - core).astype(BF16)
        copy = pltpu.make_async_remote_copy(
            src_ref=give.at[k], dst_ref=got.at[k], send_sem=core_send.at[k], recv_sem=core_recv.at[k],
            device_id=device(partner), device_id_type=MESH,
        )
        copy.start()
        core_copies.append(copy)

    stat_copy.wait()
    own_last, peer_last = own_stat[128:129, :], peer_stat[128:129, :]
    low_row = lanes((1, 128)) < 64
    both = jnp.where(low_row, own_last, pltpu.roll(peer_last, 64, 1))
    shift_row = pltpu.roll(own_last + peer_last, 64, 1)

    copies = []
    for k, offset in enumerate(OFFSETS):
        to = chip_at(offset)
        at = to * 4 + core * 2
        stat_out[k, 0:2, :] = own_stat[pl.ds(at, 2), :]
        stat_out[k, 2:4, :] = peer_stat[pl.ds(at, 2), :]
        stat_out[k, 4:6, :] = own_stat[pl.ds(at + 64, 2), :] + peer_stat[pl.ds(at + 64, 2), :]
        stat_out[k, 6:7, :] = both
        stat_out[k, 7:8, :] = shift_row
        core_copies[k].wait_recv()
        merged = gathered(to, core) + got[k].astype(F32)
        if k == CHIPS - 1:
            kept[...] = merged
            stat_in[k] = stat_out[k]
            continue
        parcel[k] = merged.astype(BF16)
        target = device(to * 2 + core)
        for src, dst, out_sem, in_sem in (
            (stat_out, stat_in, ssend_sem, srecv_sem),
            (parcel, arrived, send_sem, recv_sem),
        ):
            copy = pltpu.make_async_remote_copy(
                src_ref=src.at[k], dst_ref=dst.at[k], send_sem=out_sem.at[k], recv_sem=in_sem.at[k],
                device_id=target, device_id_type=MESH,
            )
            copy.start()
            copies.append(copy)

    for copy in copies:
        copy.wait_recv()
    total = kept[...]
    for k in range(CHIPS - 1):
        total = total + arrived[k].astype(F32)

    stat = stat_in[...]
    summed = jnp.sum(stat, axis=0)
    row_of = rows((128, 128))
    line = lax.rem(row_of, 8)
    mean_even = (summed[0:1] + summed[2:3]) * (1.0 / FEATS)
    mean_odd = (summed[1:2] + summed[3:4]) * (1.0 / FEATS)
    rstd_even = lax.rsqrt(summed[4:5] * (1.0 / FEATS) - mean_even * mean_even + 1e-06)
    rstd_odd = lax.rsqrt(summed[5:6] * (1.0 / FEATS) - mean_odd * mean_odd + 1e-06)
    offcentre = stat.reshape(128, 128) * (1.0 / LOCAL) - jnp.where(lax.rem(row_of, 2) == 0, mean_even, mean_odd)
    offcentre = jnp.where(line < 4, offcentre, 0.0)
    heads = jnp.broadcast_to(stat[:, 6:7, :], (CHIPS, 8, 128)).reshape(128, 128)
    swapped = pltpu.roll(heads, 64, 1)
    left_half = lanes((128, 128)) < 64
    zero = jnp.zeros((128, 128), F32)
    heads = jnp.where(
        line == 0, jnp.where(left_half, heads, zero),
        jnp.where(
            line == 1, jnp.where(left_half, zero, swapped),
            jnp.where(
                line == 2, jnp.where(left_half, swapped, zero),
                jnp.where(line == 3, jnp.where(left_half, zero, heads), zero),
            ),
        ),
    )
    centre = jnp.dot(jnp.transpose(heads), offcentre, precision=lax.Precision.HIGHEST, preferred_element_type=F32)
    bias = summed[7:8] + jnp.concatenate([head_b_ref[...].reshape(1, 64), jnp.zeros((1, 64), F32)], axis=1)
    bias = jnp.where(low_row, bias, pltpu.roll(bias, 64, 1))
    std = tile16(lat_std_ref[...].reshape(1, 16))
    mean = tile16(lat_mean_ref[...].reshape(1, 16))
    patches = (jnp.transpose(total) + centre) * jnp.where(row_of < 64, rstd_even, rstd_odd) + to_column(bias)
    latent = (patches * to_column(std) + to_column(mean)).astype(BF16)
    strip[1] = latent[0:64]
    strip[2] = latent[64:128]
    halos = []
    for src, dst, to in ((1, 3, left), (2, 0, right)):
        copy = pltpu.make_async_remote_copy(
            src_ref=strip.at[src], dst_ref=strip.at[dst], send_sem=halo_sem.at[src], recv_sem=halo_sem.at[dst],
            device_id=device(to), device_id_type=MESH,
        )
        copy.start()
        halos.append(copy)
    out_ref[1] = latent[0:64]
    out_ref[2] = latent[64:128]
    for copy in halos:
        copy.wait_recv()
    out_ref[0] = jnp.where(me == 0, 0.0, strip[0].astype(F32)).astype(BF16)
    out_ref[3] = jnp.where(me == GROUP - 1, 0.0, strip[3].astype(F32)).astype(BF16)
    for copy in core_copies + copies + halos:
        copy.wait_send()


def conv_kernel(
    lat_ref, conv_w_ref, conv_b_ref, up_w_ref, up_b_ref,
    out_hbm,
    taps, weight, phases, wide, stage, ready, out_sem,
):
    me = lax.axis_index("sp")
    lane = lanes((64, 128))
    frame = lax.rem(lane // 8, 8)
    half_row = lax.rem(lane, 8)

    for dx in range(3):
        for j in range(4):
            for kt in range(3):
                at = ((dx * 4 + j) * 3 + kt) * 16
                for q in range(2):
                    inside = 0 <= j - q <= 2
                    tap = conv_w_ref[kt, j - q, dx] if inside else jnp.zeros((16, 384), BF16)
                    weight[at : at + 16, q * 384 : (q + 1) * 384] = tap

    for w in range(4):
        x = lat_ref[w].astype(F32)
        above = jnp.where(lane >= 64, pltpu.roll(x, 64, 1), jnp.where(half_row == 0, 0.0, pltpu.roll(x, 65, 1)))
        below = jnp.where(lane < 64, pltpu.roll(x, 64, 1), jnp.where(half_row == 7, 0.0, pltpu.roll(x, 63, 1)))
        for kt in range(3):
            back = 2 - kt

            def earlier(v):
                if back == 0:
                    return v.astype(BF16)
                return jnp.where(frame >= back, pltpu.roll(v, 8 * back, 1), 0.0).astype(BF16)

            up, here, down = earlier(above), earlier(x), earlier(below)
            for r in range(2):
                for j, (source, q) in enumerate(((up, 1), (here, 0), (here, 1), (down, 0))):
                    at = (((w * 2 + r) * 4 + j) * 3 + kt) * 16
                    taps[at : at + 16, :] = source[q * 32 + r * 16 : q * 32 + r * 16 + 16, :]

    conv_b = conv_b_ref[...].reshape(1, 384)
    conv_b = jnp.concatenate([conv_b, conv_b], axis=1)
    inner = rows((8, 8, 384))
    for m in range(6):
        hidden = lax.dot_general(
            taps[192 * m : 192 * m + 576, :], weight[...], (((0,), (0,)), ((), ())), preferred_element_type=F32
        )
        hidden = hidden + conv_b
        if m == 0:
            hidden = jnp.where(me == 0, 0.0, hidden)
        if m == 5:
            hidden = jnp.where(me == GROUP - 1, 0.0, hidden)
        first, second = hidden[:, 0:384], hidden[:, 384:768]
        before = jnp.where(inner == 0, 0.0, pltpu.roll(second[64:128].reshape(8, 8, 384), 1, 1)).reshape(64, 384)
        after = jnp.where(inner == 7, 0.0, pltpu.roll(first[0:64].reshape(8, 8, 384), 7, 1)).reshape(64, 384)
        at = slice(128 * m, 128 * m + 128)
        wide[at, 0:384] = jnp.concatenate([before, second[0:64]], axis=0).astype(BF16)
        wide[at, 384:768] = first.astype(BF16)
        wide[at, 768:1152] = second.astype(BF16)
        wide[at, 1152:1536] = jnp.concatenate([first[64:128], after], axis=0).astype(BF16)

    def split(first, middle, last):
        return {(0, 0): first, (0, 1): middle + last, (1, 0): first + middle, (1, 1): last}

    def part(i, carry):
        at = pl.multiple_of(i * 32, 32)
        by_column = [
            split(*(up_w_ref[dy, dx, pl.ds(at, 32), :].astype(F32) for dy in range(3))) for dx in range(3)
        ]
        for a in range(2):
            for alpha in range(2):
                combined = split(*(by_column[dx][a, alpha] for dx in range(3)))
                for b in range(2):
                    for beta in range(2):
                        value = combined[b, beta].astype(BF16)
                        row = pl.multiple_of(alpha * 384 + at, 32)
                        phases[a, b, beta, pl.ds(row, 32), 0:192] = value
                        phases[a, b, beta, pl.ds(row, 32), 192:256] = jnp.zeros((32, 64), BF16)
        return carry

    lax.fori_loop(0, 12, part, 0)

    up_b = jnp.concatenate([up_b_ref[...].reshape(1, 192), jnp.zeros((1, 64), F32)], axis=1)
    copies = []
    for p in range(4):
        q, a = p // 2, p % 2
        band = slice((q + a) * 384, (q + a) * 384 + 768)
        for b in range(2):
            value = jnp.dot(wide[b * 128 : b * 128 + 512, band], phases[a, b, 0], preferred_element_type=F32)
            value += jnp.dot(wide[b * 128 + 128 : b * 128 + 640, band], phases[a, b, 1], preferred_element_type=F32)
            value = value + up_b
            for x in range(4):
                for half in range(2):
                    stage[half, pl.ds(2 * x + b, 128, stride=8), :] = value[
                        x * 128 : (x + 1) * 128, half * 128 : (half + 1) * 128
                    ]
        ready[p, :, :, 0:128] = stage[0].reshape(128, 8, 128).astype(BF16)
        ready[p, :, :, 128:192] = stage[1].reshape(128, 8, 128)[:, :, 0:64].astype(BF16)
        for parity in range(2):
            copy = pltpu.make_async_copy(
                ready.at[p, pl.ds(parity * 64, 64)], out_hbm.at[:, parity, p], out_sem.at[p, parity]
            )
            copy.start()
            copies.append(copy)
    for copy in copies:
        copy.wait()


def shards(
    hidden_feats, mod_shift, mod_scale, head_w, head_b, latent_mean, latent_std, conv_in_w, conv_in_b, up_w, up_b
):
    vmem = pl.BlockSpec(memory_space=pltpu.VMEM)
    anywhere = pl.BlockSpec(memory_space=pl.ANY)
    dma = pltpu.SemaphoreType.DMA
    latent = pl.pallas_call(
        head_kernel,
        out_shape=jax.ShapeDtypeStruct((4, 64, 128), BF16),
        in_specs=[anywhere] + [vmem] * 6,
        out_specs=vmem,
        scratch_shapes=[
            pltpu.VMEM((FRAMES, 1024, LOCAL), BF16),
            pltpu.VMEM((8192, 128), F32),
            pltpu.VMEM((64, 128), F32),
            pltpu.VMEM((64, 128), F32),
            pltpu.VMEM((136, 128), F32),
            pltpu.VMEM((136, 128), F32),
            pltpu.VMEM((CHIPS, 128, 128), BF16),
            pltpu.VMEM((CHIPS, 128, 128), BF16),
            pltpu.VMEM((128, 128), F32),
            pltpu.VMEM((CHIPS - 1, 128, 128), BF16),
            pltpu.VMEM((CHIPS - 1, 128, 128), BF16),
            pltpu.VMEM((CHIPS, 8, 128), F32),
            pltpu.VMEM((CHIPS, 8, 128), F32),
            pltpu.VMEM((4, 64, 128), BF16),
            dma((FRAMES,)),
            dma((2,)),
            dma((CHIPS,)),
            dma((CHIPS,)),
            dma((CHIPS,)),
            dma((CHIPS,)),
            dma((CHIPS,)),
            dma((CHIPS,)),
            dma((4,)),
        ],
        compiler_params=pltpu.CompilerParams(
            collective_id=0, has_side_effects=True, vmem_limit_bytes=40 * 1024 * 1024
        ),
        name="head",
    )(hidden_feats, mod_shift, mod_scale, head_w, head_b, latent_mean, latent_std)
    decoded = pl.pallas_call(
        conv_kernel,
        out_shape=jax.ShapeDtypeStruct((64, 2, 4, 8, 192), BF16),
        in_specs=[vmem] * 5,
        out_specs=anywhere,
        scratch_shapes=[
            pltpu.VMEM((8 * 192, 128), BF16),
            pltpu.VMEM((576, 768), BF16),
            pltpu.VMEM((2, 2, 2, 768, 256), BF16),
            pltpu.VMEM((768, 1536), BF16),
            pltpu.VMEM((2, 1024, 128), F32),
            pltpu.VMEM((4, 128, 8, 192), BF16),
            dma((4, 2)),
        ],
        compiler_params=pltpu.CompilerParams(vmem_limit_bytes=40 * 1024 * 1024),
        name="conv",
    )(latent, conv_in_w, conv_in_b, up_w, up_b)
    return decoded.reshape(8, 64, 8, 192)


def solution(mesh):
    placed = (
        P("req", "sp"),
        P(("req", "sp")),
        P(("req", "sp")),
        P("sp", None),
        P(),
        P(),
        P(),
        P(),
        P(),
        P(),
        P(),
    )
    return jax.shard_map(
        shards, mesh=mesh, in_specs=placed, out_specs=P("req", None, "sp", None), check_vma=False
    )
```

```python
import jax
import jax.numpy as jnp
from jax import lax
from jax.experimental import pallas as pl
from jax.experimental.pallas import tpu as pltpu
from jax.sharding import PartitionSpec as P

F32 = jnp.float32
BF16 = jnp.bfloat16
MESH = pl.DeviceIdType.MESH

FEATS = 5120
LOCAL = 160
CHUNKS = 4
CHIPS = 16
GROUP = 32
OFFSETS = [(dy, dz) for dz in (4, 3, 5, 2, 6, 1, 7) for dy in (1, 0)] + [(1, 0), (0, 0)]
NT = (((1,), (1,)), ((), ()))


def lanes(shape):
    return lax.broadcasted_iota(jnp.int32, shape, len(shape) - 1)


def rows(shape):
    return lax.broadcasted_iota(jnp.int32, shape, len(shape) - 2)


def square(width):
    return rows((width, width)) == lanes((width, width))


def to_column(row):
    return jnp.sum(jnp.where(square(row.shape[1]), row, 0.0), axis=1, keepdims=True)


def to_row(column):
    return jnp.sum(jnp.where(square(column.shape[0]), column, 0.0), axis=0, keepdims=True)


def tile16(row):
    wide = jnp.concatenate([row, jnp.zeros((1, 112), F32)], axis=1)
    for step in (16, 32, 64):
        wide = wide + pltpu.roll(wide, step, 1)
    return wide[:, 0:64]


def prepare_first(conv_w, first_w):
    for dx in range(3):
        for kt in range(3):
            for j in range(4):
                at = (kt * 4 + j) * 16
                for q in range(2):
                    inside = 0 <= j - q <= 2
                    tap = conv_w[kt, j - q, dx] if inside else jnp.zeros((16, 384), BF16)
                    first_w[dx, at : at + 16, q * 384 : (q + 1) * 384] = tap
        first_w[dx, 192:256, :] = jnp.zeros((64, 768), BF16)


def prepare_second(up_w, second_w):
    def split(first, middle, last):
        return {(0, 0): first, (0, 1): middle + last, (1, 0): first + middle, (1, 1): last}

    def part(i, carry):
        at = pl.ds(pl.multiple_of(i * 16, 16), 16)
        by_column = [split(*(up_w[dy, dx, at, :].astype(F32) for dy in range(3))) for dx in range(3)]
        for a in range(2):
            for alpha in range(2):
                combined = split(*(by_column[dx][a, alpha] for dx in range(3)))
                for b in range(2):
                    for beta in range(2):
                        second_w[a, b, beta, at, alpha * 384 : (alpha + 1) * 384] = combined[b, beta].astype(BF16)
        return carry

    lax.fori_loop(0, 12, part, 0)
    for a in range(2):
        for b in range(2):
            for beta in range(2):
                second_w[a, b, beta, 192:256, :] = jnp.zeros((64, 768), BF16)


def convolve(c, me, latent, previous, first_w, conv_b, second_w, up_b, taps, wide, stage, ready):
    lane = lanes((64, 128))
    parity, frame, half_row = lax.rem(lane // 16, 2), lax.rem(lane // 8, 2), lax.rem(lane, 8)
    above = jnp.where(parity == 1, pltpu.roll(latent, 16, 1), jnp.where(half_row == 0, 0.0, pltpu.roll(latent, 113, 1)))
    below = jnp.where(parity == 0, pltpu.roll(latent, 112, 1), jnp.where(half_row == 7, 0.0, pltpu.roll(latent, 15, 1)))
    for r in range(2):
        at = slice(r * 16, r * 16 + 16)
        low = slice(32 + r * 16, 48 + r * 16)
        now = jnp.concatenate([above[low], latent[at], latent[low], below[at]], axis=0)
        before = previous[r]
        last = jnp.where(frame == 1, pltpu.roll(now, 8, 1), pltpu.roll(before, 120, 1))
        previous[r] = now
        one = jnp.transpose(jnp.concatenate([before, last], axis=0))
        two = jnp.transpose(jnp.concatenate([now, jnp.zeros((64, 128), F32)], axis=0))
        for place, w in enumerate((1, 2, 0, 3)):
            u = 2 * w + r
            part = slice(place * 32, place * 32 + 32)
            taps[u * 32 : u * 32 + 32, 0:128] = one[part].astype(BF16)
            taps[u * 32 : u * 32 + 32, 128:256] = two[part].astype(BF16)

    inner = rows((2, 8, 384))
    whole = conv_b
    for dx in range(3):
        whole = whole + jnp.dot(taps[dx * 32 : dx * 32 + 192, :], first_w[dx], preferred_element_type=F32)
    for m in range(6):
        hidden = whole[m * 32 : m * 32 + 32]
        if m == 0:
            hidden = jnp.where(me == 0, 0.0, hidden)
        if m == 5:
            hidden = jnp.where(me == GROUP - 1, 0.0, hidden)
        upper, lower = hidden[:, 0:384], hidden[:, 384:768]
        over = jnp.where(inner == 0, 0.0, pltpu.roll(lower[16:32].reshape(2, 8, 384), 1, 1)).reshape(16, 384)
        under = jnp.where(inner == 7, 0.0, pltpu.roll(upper[0:16].reshape(2, 8, 384), 7, 1)).reshape(16, 384)
        at = slice(m * 32, m * 32 + 32)
        over = jnp.concatenate([over, lower[0:16]], axis=0).astype(BF16)
        under = jnp.concatenate([upper[16:32], under], axis=0).astype(BF16)
        upper, lower = upper.astype(BF16), lower.astype(BF16)
        for q, parts in enumerate(((over, upper, lower), (upper, lower, under))):
            for i, value in enumerate(parts):
                wide[q, at, i * 384 : (i + 1) * 384] = value

    for a in range(2):
        for b in range(2):
            value = up_b
            for beta in range(2):
                left = wide[:, (b + beta) * 32 : (b + beta) * 32 + 128, a * 384 : a * 384 + 768].reshape(256, 768)
                value = value + lax.dot_general(left, second_w[a, b, beta], NT, preferred_element_type=F32)
            for q in range(2):
                for x in range(4):
                    at = (q * 4 + x) * 32
                    for half in range(2):
                        stage[half, pl.ds((q * 2 + a) * 256 + 2 * x + b, 32, stride=8), :] = value[
                            at : at + 32, half * 128 : (half + 1) * 128
                        ]
    for p in range(4):
        for parity in range(2):
            for f in range(2):
                at = pl.ds(p * 256 + parity * 128 + f * 64, 64)
                ready[c, f, :, parity, p, :, 0:128] = stage[0, at, :].reshape(8, 8, 128).astype(BF16)
                ready[c, f, :, parity, p, :, 128:192] = stage[1, at, :].reshape(8, 8, 128)[:, :, 0:64].astype(BF16)


def kernel(
    x_hbm, shift_ref, scale_ref, head_w_ref, head_b_ref, lat_mean_ref, lat_std_ref,
    conv_w_ref, conv_b_ref, up_w_ref, up_b_ref,
    out_hbm,
    x_buf, partial, sums, turned, own_stat, peer_stat, rest, give, got, parcel, arrived, stat_out, stat_in,
    sent, beside, conv_w, up_w, first_w, second_w, previous, taps, wide, stage, ready,
    x_sem, w_sem, stat_sem, core_send, core_recv, send_sem, recv_sem, ssend_sem, srecv_sem, hsend_sem, hrecv_sem,
    out_sem,
):
    me = lax.axis_index("sp")
    req = lax.axis_index("req")
    core = lax.rem(me, 2)
    chip = me // 2
    y, z = chip // 8, lax.rem(chip, 8)
    chips = [lax.rem(y + dy, 2) * 8 + lax.rem(z + dz, 8) for dy, dz in OFFSETS]
    partner = (req, chip * 2 + (1 - core))
    left, right = lax.rem(me + GROUP - 1, GROUP), lax.rem(me + 1, GROUP)
    other = jnp.where(core == 0, left, right)

    def remote(src, dst, send, recv, to):
        return pltpu.make_async_remote_copy(
            src_ref=src, dst_ref=dst, send_sem=send, recv_sem=recv, device_id=to, device_id_type=MESH
        )

    x_copies = []
    for c in range(CHUNKS):
        copy = pltpu.make_async_copy(x_hbm.at[:, pl.ds(c * 2048, 2048)], x_buf.at[c], x_sem.at[c])
        copy.start()
        x_copies.append(copy)
    conv_copy = pltpu.make_async_copy(conv_w_ref, conv_w, w_sem.at[0])
    up_copy = pltpu.make_async_copy(up_w_ref, up_w, w_sem.at[1])
    conv_copy.start()
    up_copy.start()

    barrier = pltpu.get_barrier_semaphore()
    for to in chips[:-1]:
        pl.semaphore_signal(barrier, inc=1, device_id=(req, to * 2 + core), device_id_type=MESH)
    pl.semaphore_signal(barrier, inc=1, device_id=partner, device_id_type=MESH)
    pl.semaphore_signal(barrier, inc=1, device_id=(req, other), device_id_type=MESH)

    head = head_w_ref[...].astype(F32)
    folded = (1.0 + scale_ref[...].reshape(1, LOCAL)) * head
    weight_sum = jnp.sum(folded, axis=1, keepdims=True)
    shifted = jnp.sum(shift_ref[...].reshape(1, LOCAL) * head, axis=1, keepdims=True)
    centred = folded - weight_sum * (1.0 / LOCAL)
    high = centred.astype(BF16)
    low = (centred - high.astype(F32)).astype(BF16)
    weights = jnp.concatenate([high, low, jnp.ones((16, LOCAL), BF16)], axis=0)

    def core_copy(c):
        return remote(give.at[c], got.at[c], core_send.at[c], core_recv.at[c], partner)

    def gathered(c, to, core_to):
        at = (to * 2 + core_to) * 2
        return jnp.concatenate(
            [
                partial[c, pl.ds(parity * 64 + at + column, 8, stride=128), :]
                for column in range(2)
                for parity in range(2)
            ],
            axis=0,
        )

    def parcel_copy(c, k):
        return remote(
            parcel.at[c, k], arrived.at[c, k], send_sem.at[c, k], recv_sem.at[c, k], (req, chips[k] * 2 + core)
        )

    def dispatch(c):
        core_copy(c).wait_recv()
        for k in range(CHIPS):
            merged = gathered(c, chips[k], core) + got[c, k].astype(F32)
            if k == CHIPS - 1:
                rest[c] = merged
            else:
                parcel[c, k] = merged.astype(BF16)
                parcel_copy(c, k).start()

    for c in range(CHUNKS):
        x_copies[c].wait()

        def block(i, carry):
            products = []
            for f in range(2):
                x = x_buf[c, :, pl.ds(pl.multiple_of(f * 1024 + i * 256, 256), 256)]
                product = jnp.dot(weights, x, preferred_element_type=F32)
                products.append(product[0:64] + product[64:128])
                wide_x = x.astype(F32)
                power = jnp.sum(wide_x * wide_x, axis=0, keepdims=True)
                for half in range(2):
                    at = (c * 2 + f) * 8 + i * 2 + half
                    cut = slice(half * 128, half * 128 + 128)
                    sums[pl.ds(at, 1), :] = product[128:129, cut]
                    sums[pl.ds(64 + at, 1), :] = power[:, cut]
            for half in range(2):
                cut = slice(half * 128, half * 128 + 128)
                pair = jnp.concatenate([products[0][:, cut], products[1][:, cut]], axis=0)
                partial[c, pl.ds(pl.multiple_of((i * 2 + half) * 128, 128), 128), :] = jnp.transpose(pair)
            return carry

        lax.fori_loop(0, 4, block, 0, unroll=True)
        if c == 0:
            pl.semaphore_wait(barrier, 17)
        for k in range(CHIPS):
            give[c, k] = gathered(c, chips[k], 1 - core).astype(BF16)
        core_copy(c).start()

    turned[0:128, :] = jnp.transpose(sums[...])
    group = lax.rem(lanes((32, 128)) // 16, 4)
    quarters = [turned[pl.ds(parity * 64 + column, 32, stride=2), :] for column in range(2) for parity in range(2)]
    for c in range(CHUNKS):
        placed = [quarters[g] if g == c else pltpu.roll(quarters[g], (16 * (g - c)) % 128, 1) for g in range(4)]
        own_stat[c] = jnp.where(
            group == 0, placed[0], jnp.where(group == 1, placed[1], jnp.where(group == 2, placed[2], placed[3]))
        )
    own_row = jnp.concatenate([to_row(weight_sum), to_row(shifted)], axis=1)
    own_stat[4] = jnp.broadcast_to(own_row, (32, 128))
    stat_copy = remote(own_stat, peer_stat, stat_sem.at[0], stat_sem.at[1], partner)
    stat_copy.start()
    dispatch(0)
    stat_copy.wait()

    low_half = lanes((32, 128)) < 64
    own = [own_stat[c] for c in range(5)]
    peer = [peer_stat[c] for c in range(5)]
    both = [own[c] + peer[c] for c in range(5)]
    turned_both = [pltpu.roll(both[c], 64, 1) for c in range(5)]
    lines = [jnp.where(low_half, own[c], pltpu.roll(peer[c], 64, 1)) for c in range(5)]
    lines = lines[0:4] + [
        jnp.where(low_half, turned_both[0], both[1]), jnp.where(low_half, turned_both[2], both[3]),
        lines[4], turned_both[4],
    ]
    for line in range(8):
        turned[pl.ds(line, 32, stride=8), :] = lines[line]

    def stat_remote(k):
        return remote(
            stat_out.at[k], stat_in.at[pl.ds(k * 8, 8)], ssend_sem.at[k], srecv_sem.at[k], (req, chips[k] * 2 + core)
        )

    for k in range(CHIPS):
        value = turned[pl.ds(pl.multiple_of((chips[k] * 2 + core) * 8, 8), 8), :]
        if k == CHIPS - 1:
            stat_in[k * 8 : k * 8 + 8, :] = value
        else:
            stat_out[k] = value
            stat_remote(k).start()

    dispatch(1)
    conv_copy.wait()
    prepare_first(conv_w, first_w)
    up_copy.wait()
    prepare_second(up_w, second_w)
    previous[...] = jnp.zeros((2, 64, 128), F32)

    for k in range(CHIPS - 1):
        stat_remote(k).wait_recv()
    total = jnp.sum(stat_in[...].reshape(CHIPS, 8, 128), axis=0)
    sums_of = [stat_in[pl.ds(c, CHIPS, stride=8), :] for c in range(4)]
    heads = stat_in[pl.ds(6, CHIPS, stride=8), :]
    heads = jnp.concatenate([heads, pltpu.roll(heads, 64, 1), jnp.zeros((96, 128), F32)], axis=0)
    heads = jnp.transpose(heads)[0:64, :]
    both_sums = total + pltpu.roll(total, 64, 1)
    means = both_sums[0:4] * (1.0 / FEATS)
    swapped = pltpu.roll(total, 64, 1)
    bias = to_column(total[7:8, 0:64] + head_b_ref[...].reshape(1, 64))
    std = to_column(tile16(lat_std_ref[...].reshape(1, 16)))
    shift = to_column(tile16(lat_mean_ref[...].reshape(1, 16)))
    centres, scales = [], []
    for c in range(CHUNKS):
        mean = means[c : c + 1]
        off = sums_of[c] * (1.0 / LOCAL) - mean
        off = jnp.concatenate([off, pltpu.roll(off, 64, 1), jnp.zeros((96, 128), F32)], axis=0)
        centres.append(jnp.dot(heads, off, precision=lax.Precision.HIGHEST, preferred_element_type=F32))
        power = (total if c % 2 == 0 else swapped)[4 + c // 2 : 5 + c // 2]
        scales.append(lax.rsqrt(power * (1.0 / FEATS) - mean * mean + 1e-06))

    lane = lanes((64, 128))
    conv_b = conv_b_ref[...].reshape(1, 384)
    conv_b = jnp.concatenate([conv_b, conv_b], axis=1)
    up_b = jnp.concatenate([up_b_ref[...].reshape(1, 192), jnp.zeros((1, 64), F32)], axis=1)

    def halo_copies(c):
        return [
            remote(sent.at[c], beside.at[c, side], hsend_sem.at[c, side], hrecv_sem.at[c, side], (req, to))
            for side, to in ((1, left), (0, right))
        ]

    def finish(c):
        for k in range(CHIPS - 1):
            parcel_copy(c, k).wait_recv()
        value = rest[c]
        for k in range(CHIPS - 1):
            value = value + arrived[c, k].astype(F32)
        none = jnp.zeros((8, 128), F32)
        spread = []
        for g in range(4):
            spread += [value[g * 8 : g * 8 + 8], none]
        value = jnp.transpose(jnp.concatenate(spread + [jnp.zeros((64, 128), F32)], axis=0))
        value = jnp.where(lax.rem(lane // 8, 2) == 0, value[0:64], pltpu.roll(value[64:128], 8, 1))
        patches = (value + centres[c]) * scales[c] + bias
        sent[c] = (patches * std + shift).astype(BF16)
        for copy in halo_copies(c):
            copy.start()

    def decode(c):
        for copy in halo_copies(c):
            copy.wait_recv()
        own = sent[c].astype(F32)
        before = jnp.where(me == 0, 0.0, pltpu.roll(beside[c, 0].astype(F32), 32, 1))
        after = jnp.where(me == GROUP - 1, 0.0, pltpu.roll(beside[c, 1].astype(F32), 96, 1))
        latent = jnp.where(lane < 64, own, jnp.where(lane < 96, before, after))
        convolve(c, me, latent, previous, first_w, conv_b, second_w, up_b, taps, wide, stage, ready)
        pltpu.make_async_copy(ready.at[c], out_hbm.at[pl.ds(2 * c, 2)], out_sem.at[c]).start()

    finish(0)
    dispatch(2)
    finish(1)
    dispatch(3)
    decode(0)
    finish(2)
    decode(1)
    finish(3)
    decode(2)
    decode(3)

    for c in range(CHUNKS):
        pltpu.make_async_copy(ready.at[c], out_hbm.at[pl.ds(2 * c, 2)], out_sem.at[c]).wait()
        core_copy(c).wait_send()
        for k in range(CHIPS - 1):
            parcel_copy(c, k).wait_send()
        for copy in halo_copies(c):
            copy.wait_send()
    for k in range(CHIPS - 1):
        stat_remote(k).wait_send()


def shards(
    hidden_feats, mod_shift, mod_scale, head_w, head_b, latent_mean, latent_std, conv_in_w, conv_in_b, up_w, up_b
):
    vmem = pl.BlockSpec(memory_space=pltpu.VMEM)
    hbm = pl.BlockSpec(memory_space=pltpu.HBM)
    dma = pltpu.SemaphoreType.DMA
    decoded = pl.pallas_call(
        kernel,
        out_shape=jax.ShapeDtypeStruct((8, 8, 2, 4, 8, 192), BF16),
        in_specs=[hbm] + [vmem] * 6 + [hbm, vmem, hbm, vmem],
        out_specs=hbm,
        scratch_shapes=[
            pltpu.VMEM((CHUNKS, LOCAL, 2048), BF16),
            pltpu.VMEM((CHUNKS, 1024, 128), F32),
            pltpu.VMEM((128, 128), F32),
            pltpu.VMEM((256, 128), F32),
            pltpu.VMEM((5, 32, 128), F32),
            pltpu.VMEM((5, 32, 128), F32),
            pltpu.VMEM((CHUNKS, 32, 128), F32),
            pltpu.VMEM((CHUNKS, CHIPS, 32, 128), BF16),
            pltpu.VMEM((CHUNKS, CHIPS, 32, 128), BF16),
            pltpu.VMEM((CHUNKS, CHIPS, 32, 128), BF16),
            pltpu.VMEM((CHUNKS, CHIPS, 32, 128), BF16),
            pltpu.VMEM((CHIPS, 8, 128), F32),
            pltpu.VMEM((CHIPS * 8, 128), F32),
            pltpu.VMEM((CHUNKS, 64, 128), BF16),
            pltpu.VMEM((CHUNKS, 2, 64, 128), BF16),
            pltpu.VMEM((3, 3, 3, 16, 384), BF16),
            pltpu.VMEM((3, 3, 192, 384), BF16),
            pltpu.VMEM((3, 256, 768), BF16),
            pltpu.VMEM((2, 2, 2, 256, 768), BF16),
            pltpu.VMEM((2, 64, 128), F32),
            pltpu.VMEM((256, 256), BF16),
            pltpu.VMEM((2, 192, 1152), BF16),
            pltpu.VMEM((2, 1024, 128), F32),
            pltpu.VMEM((CHUNKS, 2, 8, 2, 4, 8, 192), BF16),
            dma((CHUNKS,)),
            dma((2,)),
            dma((2,)),
            dma((CHUNKS,)),
            dma((CHUNKS,)),
            dma((CHUNKS, CHIPS)),
            dma((CHUNKS, CHIPS)),
            dma((CHIPS,)),
            dma((CHIPS,)),
            dma((CHUNKS, 2)),
            dma((CHUNKS, 2)),
            dma((CHUNKS,)),
        ],
        compiler_params=pltpu.CompilerParams(
            collective_id=0, has_side_effects=True, vmem_limit_bytes=62 * 1024 * 1024
        ),
        name="decode",
    )(
        hidden_feats.T, mod_shift, mod_scale, head_w.T, head_b, latent_mean, latent_std,
        conv_in_w, conv_in_b, jnp.swapaxes(up_w, 2, 3), up_b,
    )
    return decoded.reshape(8, 64, 8, 192)


def solution(mesh):
    placed = (
        P("req", "sp"),
        P(("req", "sp")),
        P(("req", "sp")),
        P("sp", None),
        P(),
        P(),
        P(),
        P(),
        P(),
        P(),
        P(),
    )
    return jax.shard_map(
        shards, mesh=mesh, in_specs=placed, out_specs=P("req", None, "sp", None), check_vma=False
    )
```

```python
import jax
import jax.numpy as jnp
from jax import lax
from jax.experimental import pallas as pl
from jax.experimental.pallas import tpu as pltpu
from jax.sharding import PartitionSpec as P

F32 = jnp.float32
BF16 = jnp.bfloat16
MESH = pl.DeviceIdType.MESH

FEATS = 5120
LOCAL = 160
CHUNKS = 4
CHIPS = 16
GROUP = 32
OFFSETS = [(dy, dz) for dz in (4, 3, 5, 2, 6, 1, 7) for dy in (1, 0)] + [(1, 0), (0, 0)]
NT = (((1,), (1,)), ((), ()))


def lanes(shape):
    return lax.broadcasted_iota(jnp.int32, shape, len(shape) - 1)


def rows(shape):
    return lax.broadcasted_iota(jnp.int32, shape, len(shape) - 2)


def square(width):
    return rows((width, width)) == lanes((width, width))


def to_column(row):
    return jnp.sum(jnp.where(square(row.shape[1]), row, 0.0), axis=1, keepdims=True)


def to_row(column):
    return jnp.sum(jnp.where(square(column.shape[0]), column, 0.0), axis=0, keepdims=True)


def tile16(row):
    wide = jnp.concatenate([row, jnp.zeros((1, 112), F32)], axis=1)
    for step in (16, 32, 64):
        wide = wide + pltpu.roll(wide, step, 1)
    return wide[:, 0:64]


def prepare_first(conv_w, first_w):
    for dx in range(3):
        for kt in range(3):
            for j in range(4):
                at = (kt * 4 + j) * 16
                for q in range(2):
                    inside = 0 <= j - q <= 2
                    tap = conv_w[kt, j - q, dx] if inside else jnp.zeros((16, 384), BF16)
                    first_w[dx, at : at + 16, q * 384 : (q + 1) * 384] = tap
        first_w[dx, 192:256, :] = jnp.zeros((64, 768), BF16)


def prepare_second(up_w, second_w):
    def split(first, middle, last):
        return {(0, 0): first, (0, 1): middle + last, (1, 0): first + middle, (1, 1): last}

    def part(i, carry):
        at = pl.ds(pl.multiple_of(i * 16, 16), 16)
        by_column = [split(*(up_w[dy, dx, at, :].astype(F32) for dy in range(3))) for dx in range(3)]
        for a in range(2):
            for alpha in range(2):
                combined = split(*(by_column[dx][a, alpha] for dx in range(3)))
                for b in range(2):
                    for beta in range(2):
                        second_w[a, b, beta, at, alpha * 384 : (alpha + 1) * 384] = combined[b, beta].astype(BF16)
        return carry

    lax.fori_loop(0, 12, part, 0)
    for a in range(2):
        for b in range(2):
            for beta in range(2):
                second_w[a, b, beta, 192:256, :] = jnp.zeros((64, 768), BF16)


def first_convolution(me, latent, previous, first_w, conv_b, taps, wide):
    lane = lanes((64, 128))
    parity, frame, half_row = lax.rem(lane // 16, 2), lax.rem(lane // 8, 2), lax.rem(lane, 8)
    above = jnp.where(parity == 1, pltpu.roll(latent, 16, 1), jnp.where(half_row == 0, 0.0, pltpu.roll(latent, 113, 1)))
    below = jnp.where(parity == 0, pltpu.roll(latent, 112, 1), jnp.where(half_row == 7, 0.0, pltpu.roll(latent, 15, 1)))
    for r in range(2):
        at = slice(r * 16, r * 16 + 16)
        low = slice(32 + r * 16, 48 + r * 16)
        now = jnp.concatenate([above[low], latent[at], latent[low], below[at]], axis=0)
        before = previous[r]
        last = jnp.where(frame == 1, pltpu.roll(now, 8, 1), pltpu.roll(before, 120, 1))
        previous[r] = now
        one = jnp.transpose(jnp.concatenate([before, last], axis=0))
        two = jnp.transpose(jnp.concatenate([now, jnp.zeros((64, 128), F32)], axis=0))
        for place, w in enumerate((1, 2, 0, 3)):
            u = 2 * w + r
            part = slice(place * 32, place * 32 + 32)
            taps[u * 32 : u * 32 + 32, 0:128] = one[part].astype(BF16)
            taps[u * 32 : u * 32 + 32, 128:256] = two[part].astype(BF16)

    inner = rows((2, 8, 384))
    whole = conv_b
    for dx in range(3):
        whole = whole + jnp.dot(taps[dx * 32 : dx * 32 + 192, :], first_w[dx], preferred_element_type=F32)
    for m in range(6):
        hidden = whole[m * 32 : m * 32 + 32]
        if m == 0:
            hidden = jnp.where(me == 0, 0.0, hidden)
        if m == 5:
            hidden = jnp.where(me == GROUP - 1, 0.0, hidden)
        upper, lower = hidden[:, 0:384], hidden[:, 384:768]
        over = jnp.where(inner == 0, 0.0, pltpu.roll(lower[16:32].reshape(2, 8, 384), 1, 1)).reshape(16, 384)
        under = jnp.where(inner == 7, 0.0, pltpu.roll(upper[0:16].reshape(2, 8, 384), 7, 1)).reshape(16, 384)
        at = slice(m * 32, m * 32 + 32)
        over = jnp.concatenate([over, lower[0:16]], axis=0).astype(BF16)
        under = jnp.concatenate([upper[16:32], under], axis=0).astype(BF16)
        upper, lower = upper.astype(BF16), lower.astype(BF16)
        for q, parts in enumerate(((over, upper, lower), (upper, lower, under))):
            for i, value in enumerate(parts):
                wide[q, at, i * 384 : (i + 1) * 384] = value


def second_convolution(second_w, up_b, wide, stage, ready, between=None):
    for a in range(2):
        if a == 1 and between is not None:
            between()
        for b in range(2):
            value = up_b
            for beta in range(2):
                left = wide[:, (b + beta) * 32 : (b + beta) * 32 + 128, a * 384 : a * 384 + 768].reshape(256, 768)
                value = value + lax.dot_general(left, second_w[a, b, beta], NT, preferred_element_type=F32)
            for q in range(2):
                for x in range(4):
                    at = (q * 4 + x) * 32
                    for half in range(2):
                        stage[half, pl.ds((q * 2 + a) * 256 + 2 * x + b, 32, stride=8), :] = value[
                            at : at + 32, half * 128 : (half + 1) * 128
                        ]
    for p in range(4):
        for parity in range(2):
            for f in range(2):
                at = pl.ds(p * 256 + parity * 128 + f * 64, 64)
                ready[f, :, parity, p, :, 0:128] = stage[0, at, :].reshape(8, 8, 128).astype(BF16)
                ready[f, :, parity, p, :, 128:192] = stage[1, at, :].reshape(8, 8, 128)[:, :, 0:64].astype(BF16)


def reduce_kernel(
    x_hbm, shift_hbm, scale_hbm, head_w_hbm, head_b_hbm, lat_mean_hbm, lat_std_hbm,
    conv_w_hbm, conv_b_hbm, up_w_hbm, up_b_hbm,
    out_hbm, state_hbm, first_hbm, second_hbm,
    x_buf, partial, sums, turned, own_stat, peer_stat, rest, give, got, parcel, arrived, stat_out, stat_in,
    sent, beside, conv_w, up_w, first_w, second_w, previous, taps, wide, stage, ready, state,
    shift_ref, scale_ref, head_w_ref, head_b_ref, lat_mean_ref, lat_std_ref, conv_b_ref, up_b_ref,
    x_sem, w_sem, stat_sem, core_send, core_recv, send_sem, recv_sem, ssend_sem, srecv_sem, hsend_sem, hrecv_sem,
    out_sem, keep_sem, small_sem,
):
    me = lax.axis_index("sp")
    req = lax.axis_index("req")
    core = lax.rem(me, 2)
    chip = me // 2
    y, z = chip // 8, lax.rem(chip, 8)
    chips = [lax.rem(y + dy, 2) * 8 + lax.rem(z + dz, 8) for dy, dz in OFFSETS]
    partner = (req, chip * 2 + (1 - core))
    left, right = lax.rem(me + GROUP - 1, GROUP), lax.rem(me + 1, GROUP)
    other = jnp.where(core == 0, left, right)

    def remote(src, dst, send, recv, to):
        return pltpu.make_async_remote_copy(
            src_ref=src, dst_ref=dst, send_sem=send, recv_sem=recv, device_id=to, device_id_type=MESH
        )

    pairs = (
        (shift_hbm, shift_ref), (scale_hbm, scale_ref), (head_w_hbm, head_w_ref), (head_b_hbm, head_b_ref),
        (lat_mean_hbm, lat_mean_ref), (lat_std_hbm, lat_std_ref), (conv_b_hbm, conv_b_ref), (up_b_hbm, up_b_ref),
    )
    small = [pltpu.make_async_copy(src, dst, small_sem.at[i]) for i, (src, dst) in enumerate(pairs)]
    for copy in small:
        copy.start()
    x_copies = []
    for c in range(CHUNKS):
        copy = pltpu.make_async_copy(x_hbm.at[:, pl.ds(c * 2048, 2048)], x_buf.at[c], x_sem.at[c])
        copy.start()
        x_copies.append(copy)

    barrier = pltpu.get_barrier_semaphore()
    for to in chips[:-1]:
        pl.semaphore_signal(barrier, inc=1, device_id=(req, to * 2 + core), device_id_type=MESH)
    pl.semaphore_signal(barrier, inc=1, device_id=partner, device_id_type=MESH)
    pl.semaphore_signal(barrier, inc=1, device_id=(req, other), device_id_type=MESH)

    conv_copy = pltpu.make_async_copy(conv_w_hbm, conv_w, w_sem.at[0])
    up_copy = pltpu.make_async_copy(up_w_hbm, up_w, w_sem.at[1])
    conv_copy.start()
    up_copy.start()

    for copy in small:
        copy.wait()
    head = head_w_ref[...].astype(F32)
    folded = (1.0 + scale_ref[...].reshape(1, LOCAL)) * head
    weight_sum = jnp.sum(folded, axis=1, keepdims=True)
    shifted = jnp.sum(shift_ref[...].reshape(1, LOCAL) * head, axis=1, keepdims=True)
    centred = folded - weight_sum * (1.0 / LOCAL)
    high = centred.astype(BF16)
    low = (centred - high.astype(F32)).astype(BF16)
    weights = jnp.concatenate([high, low, jnp.ones((16, LOCAL), BF16)], axis=0)

    def core_copy(c):
        return remote(give.at[c], got.at[c], core_send.at[c], core_recv.at[c], partner)

    def gathered(c, to, core_to):
        at = (to * 2 + core_to) * 2
        return jnp.concatenate(
            [
                partial[c, pl.ds(parity * 64 + at + column, 8, stride=128), :]
                for column in range(2)
                for parity in range(2)
            ],
            axis=0,
        )

    def parcel_copy(c, k):
        return remote(
            parcel.at[c, k], arrived.at[c, k], send_sem.at[c, k], recv_sem.at[c, k], (req, chips[k] * 2 + core)
        )

    def dispatch(c):
        core_copy(c).wait_recv()
        for k in range(CHIPS):
            merged = gathered(c, chips[k], core) + got[c, k].astype(F32)
            if k == CHIPS - 1:
                rest[c] = merged
            else:
                parcel[c, k] = merged.astype(BF16)
                parcel_copy(c, k).start()

    for c in range(CHUNKS):
        x_copies[c].wait()

        def block(i, carry):
            products = []
            for f in range(2):
                x = x_buf[c, :, pl.ds(pl.multiple_of(f * 1024 + i * 256, 256), 256)]
                product = jnp.dot(weights, x, preferred_element_type=F32)
                products.append(product[0:64] + product[64:128])
                wide_x = x.astype(F32)
                power = jnp.sum(wide_x * wide_x, axis=0, keepdims=True)
                for half in range(2):
                    at = (c * 2 + f) * 8 + i * 2 + half
                    cut = slice(half * 128, half * 128 + 128)
                    sums[pl.ds(at, 1), :] = product[128:129, cut]
                    sums[pl.ds(64 + at, 1), :] = power[:, cut]
            for half in range(2):
                cut = slice(half * 128, half * 128 + 128)
                pair = jnp.concatenate([products[0][:, cut], products[1][:, cut]], axis=0)
                partial[c, pl.ds(pl.multiple_of((i * 2 + half) * 128, 128), 128), :] = jnp.transpose(pair)
            return carry

        lax.fori_loop(0, 4, block, 0, unroll=True)
    pl.semaphore_wait(barrier, 17)
    for c in range(CHUNKS):
        for k in range(CHIPS):
            give[c, k] = gathered(c, chips[k], 1 - core).astype(BF16)
        core_copy(c).start()

    turned[0:128, :] = jnp.transpose(sums[...])
    group = lax.rem(lanes((32, 128)) // 16, 4)
    quarters = [turned[pl.ds(parity * 64 + column, 32, stride=2), :] for column in range(2) for parity in range(2)]
    for c in range(CHUNKS):
        placed = [quarters[g] if g == c else pltpu.roll(quarters[g], (16 * (g - c)) % 128, 1) for g in range(4)]
        own_stat[c] = jnp.where(
            group == 0, placed[0], jnp.where(group == 1, placed[1], jnp.where(group == 2, placed[2], placed[3]))
        )
    own_row = jnp.concatenate([to_row(weight_sum), to_row(shifted)], axis=1)
    own_stat[4] = jnp.broadcast_to(own_row, (32, 128))
    stat_copy = remote(own_stat, peer_stat, stat_sem.at[0], stat_sem.at[1], partner)
    stat_copy.start()
    dispatch(0)
    stat_copy.wait()

    low_half = lanes((32, 128)) < 64
    own = [own_stat[c] for c in range(5)]
    peer = [peer_stat[c] for c in range(5)]
    both = [own[c] + peer[c] for c in range(5)]
    turned_both = [pltpu.roll(both[c], 64, 1) for c in range(5)]
    lines = [jnp.where(low_half, own[c], pltpu.roll(peer[c], 64, 1)) for c in range(5)]
    lines = lines[0:4] + [
        jnp.where(low_half, turned_both[0], both[1]), jnp.where(low_half, turned_both[2], both[3]),
        lines[4], turned_both[4],
    ]
    for line in range(8):
        turned[pl.ds(line, 32, stride=8), :] = lines[line]

    def stat_remote(k):
        return remote(
            stat_out.at[k], stat_in.at[pl.ds(k * 8, 8)], ssend_sem.at[k], srecv_sem.at[k], (req, chips[k] * 2 + core)
        )

    for k in range(CHIPS):
        value = turned[pl.ds(pl.multiple_of((chips[k] * 2 + core) * 8, 8), 8), :]
        if k == CHIPS - 1:
            stat_in[k * 8 : k * 8 + 8, :] = value
        else:
            stat_out[k] = value
            stat_remote(k).start()

    dispatch(1)
    dispatch(2)
    conv_copy.wait()
    prepare_first(conv_w, first_w)
    up_copy.wait()
    prepare_second(up_w, second_w)
    previous[...] = jnp.zeros((2, 64, 128), F32)
    keeps = [
        pltpu.make_async_copy(first_w, first_hbm, keep_sem.at[0]),
        pltpu.make_async_copy(second_w, second_hbm, keep_sem.at[1]),
    ]
    for copy in keeps:
        copy.start()

    for k in range(CHIPS - 1):
        stat_remote(k).wait_recv()
    total = jnp.sum(stat_in[...].reshape(CHIPS, 8, 128), axis=0)
    sums_of = [stat_in[pl.ds(c, CHIPS, stride=8), :] for c in range(4)]
    heads = stat_in[pl.ds(6, CHIPS, stride=8), :]
    heads = jnp.concatenate([heads, pltpu.roll(heads, 64, 1), jnp.zeros((96, 128), F32)], axis=0)
    heads = jnp.transpose(heads)[0:64, :]
    both_sums = total + pltpu.roll(total, 64, 1)
    means = both_sums[0:4] * (1.0 / FEATS)
    swapped = pltpu.roll(total, 64, 1)
    bias = to_column(total[7:8, 0:64] + head_b_ref[...].reshape(1, 64))
    std = to_column(tile16(lat_std_ref[...].reshape(1, 16)))
    shift = to_column(tile16(lat_mean_ref[...].reshape(1, 16)))
    centres, scales = [], []
    for c in range(CHUNKS):
        mean = means[c : c + 1]
        off = sums_of[c] * (1.0 / LOCAL) - mean
        off = jnp.concatenate([off, pltpu.roll(off, 64, 1), jnp.zeros((96, 128), F32)], axis=0)
        centres.append(jnp.dot(heads, off, precision=lax.Precision.HIGHEST, preferred_element_type=F32))
        power = (total if c % 2 == 0 else swapped)[4 + c // 2 : 5 + c // 2]
        scales.append(lax.rsqrt(power * (1.0 / FEATS) - mean * mean + 1e-06))

    lane = lanes((64, 128))
    conv_b = conv_b_ref[...].reshape(1, 384)
    conv_b = jnp.concatenate([conv_b, conv_b], axis=1)
    up_b = jnp.concatenate([up_b_ref[...].reshape(1, 192), jnp.zeros((1, 64), F32)], axis=1)

    def halo_copies(c):
        return [
            remote(sent.at[c], beside.at[c, side], hsend_sem.at[c, side], hrecv_sem.at[c, side], (req, to))
            for side, to in ((1, left), (0, right))
        ]

    def ends(c, action):
        to_left, to_right = halo_copies(c)
        pl.when(me > 0)(getattr(to_left, action))
        pl.when(me < GROUP - 1)(getattr(to_right, action))

    def finish(c):
        for k in range(CHIPS - 1):
            parcel_copy(c, k).wait_recv()
        value = rest[c]
        for k in range(CHIPS - 1):
            value = value + arrived[c, k].astype(F32)
        none = jnp.zeros((8, 128), F32)
        spread = []
        for g in range(4):
            spread += [value[g * 8 : g * 8 + 8], none]
        value = jnp.transpose(jnp.concatenate(spread + [jnp.zeros((64, 128), F32)], axis=0))
        value = jnp.where(lax.rem(lane // 8, 2) == 0, value[0:64], pltpu.roll(value[64:128], 8, 1))
        patches = (value + centres[c]) * scales[c] + bias
        sent[c] = (patches * std + shift).astype(BF16)
        ends(c, "start")

    def assembled(c):
        pl.when(me > 0)(halo_copies(c)[1].wait_recv)
        pl.when(me < GROUP - 1)(halo_copies(c)[0].wait_recv)
        own = sent[c].astype(F32)
        before = jnp.where(me == 0, 0.0, pltpu.roll(beside[c, 0].astype(F32), 32, 1))
        after = jnp.where(me == GROUP - 1, 0.0, pltpu.roll(beside[c, 1].astype(F32), 96, 1))
        return jnp.where(lane < 64, own, jnp.where(lane < 96, before, after))

    def out_copy(c):
        return pltpu.make_async_copy(ready.at[c], out_hbm.at[pl.ds(2 * c, 2)], out_sem.at[c])

    def decode(c):
        latent = assembled(c)
        first_convolution(me, latent, previous, first_w, conv_b, taps, wide)
        second_convolution(second_w, up_b, wide, stage, ready.at[c])
        out_copy(c).start()

    finish(0)
    dispatch(3)
    finish(1)
    decode(0)
    finish(2)
    decode(1)
    finish(3)
    decode(2)

    state[2] = assembled(CHUNKS - 1)
    state[0:2] = previous[...]
    for i in range(6):
        state[3, i : i + 1, :] = conv_b[:, i * 128 : (i + 1) * 128]
    for i in range(2):
        state[3, 8 + i : 9 + i, :] = up_b[:, i * 128 : (i + 1) * 128]
    keeps.append(pltpu.make_async_copy(state, state_hbm, keep_sem.at[2]))
    keeps[2].start()
    for c in range(CHUNKS):
        if c < CHUNKS - 1:
            out_copy(c).wait()
        core_copy(c).wait_send()
        for k in range(CHIPS - 1):
            parcel_copy(c, k).wait_send()
        ends(c, "wait_send")
    for k in range(CHIPS - 1):
        stat_remote(k).wait_send()
    for copy in keeps:
        copy.wait()


def last_kernel(
    done_hbm, state_hbm, first_hbm, second_hbm,
    out_hbm,
    done, state, first_w, second_w, previous, taps, wide, stage, ready, sem,
):
    me = lax.axis_index("sp")
    frames = 2 * (CHUNKS - 1)
    load_state = pltpu.make_async_copy(state_hbm, state, sem.at[0])
    load_first = pltpu.make_async_copy(first_hbm, first_w, sem.at[1])
    load_second = pltpu.make_async_copy(second_hbm, second_w, sem.at[2])
    load_done = pltpu.make_async_copy(done_hbm, done, sem.at[3])
    for copy in (load_state, load_first, load_second, load_done):
        copy.start()
    load_state.wait()
    previous[...] = state[0:2]
    conv_b = jnp.concatenate([state[3, i : i + 1, :] for i in range(6)], axis=1)
    up_b = jnp.concatenate([state[3, i : i + 1, :] for i in (8, 9)], axis=1)
    load_first.wait()
    first_convolution(me, state[2], previous, first_w, conv_b, taps, wide)
    load_second.wait()
    store_done = pltpu.make_async_copy(done, out_hbm.at[pl.ds(0, frames)], sem.at[4])

    def between():
        load_done.wait()
        store_done.start()

    second_convolution(second_w, up_b, wide, stage, ready, between)
    store = pltpu.make_async_copy(ready, out_hbm.at[pl.ds(frames, 2)], sem.at[5])
    store.start()
    store_done.wait()
    store.wait()


def shards(
    hidden_feats, mod_shift, mod_scale, head_w, head_b, latent_mean, latent_std, conv_in_w, conv_in_b, up_w, up_b
):
    hbm = pl.BlockSpec(memory_space=pltpu.HBM)
    dma = pltpu.SemaphoreType.DMA
    pieces = jax.ShapeDtypeStruct((8, 8, 2, 4, 8, 192), BF16)
    work = [
        pltpu.VMEM((2, 64, 128), F32),
        pltpu.VMEM((256, 256), BF16),
        pltpu.VMEM((2, 192, 1152), BF16),
        pltpu.VMEM((2, 1024, 128), F32),
    ]
    held = [
        jax.ShapeDtypeStruct((4, 64, 128), F32),
        jax.ShapeDtypeStruct((3, 256, 768), BF16),
        jax.ShapeDtypeStruct((2, 2, 2, 256, 768), BF16),
    ]
    done, state, first_w, second_w = pl.pallas_call(
        reduce_kernel,
        out_shape=[jax.ShapeDtypeStruct((6, 8, 2, 4, 8, 192), BF16)] + held,
        in_specs=[hbm] * 11,
        out_specs=[hbm] * 4,
        scratch_shapes=[
            pltpu.VMEM((CHUNKS, LOCAL, 2048), BF16),
            pltpu.VMEM((CHUNKS, 1024, 128), F32),
            pltpu.VMEM((128, 128), F32),
            pltpu.VMEM((256, 128), F32),
            pltpu.VMEM((5, 32, 128), F32),
            pltpu.VMEM((5, 32, 128), F32),
            pltpu.VMEM((CHUNKS, 32, 128), F32),
            pltpu.VMEM((CHUNKS, CHIPS, 32, 128), BF16),
            pltpu.VMEM((CHUNKS, CHIPS, 32, 128), BF16),
            pltpu.VMEM((CHUNKS, CHIPS, 32, 128), BF16),
            pltpu.VMEM((CHUNKS, CHIPS, 32, 128), BF16),
            pltpu.VMEM((CHIPS, 8, 128), F32),
            pltpu.VMEM((CHIPS * 8, 128), F32),
            pltpu.VMEM((CHUNKS, 64, 128), BF16),
            pltpu.VMEM((CHUNKS, 2, 64, 128), BF16),
            pltpu.VMEM((3, 3, 3, 16, 384), BF16),
            pltpu.VMEM((3, 3, 192, 384), BF16),
            pltpu.VMEM((3, 256, 768), BF16),
            pltpu.VMEM((2, 2, 2, 256, 768), BF16),
            *work,
            pltpu.VMEM((CHUNKS - 1, 2, 8, 2, 4, 8, 192), BF16),
            pltpu.VMEM((4, 64, 128), F32),
            pltpu.VMEM((LOCAL,), F32),
            pltpu.VMEM((LOCAL,), F32),
            pltpu.VMEM((64, LOCAL), BF16),
            pltpu.VMEM((64,), F32),
            pltpu.VMEM((16,), F32),
            pltpu.VMEM((16,), F32),
            pltpu.VMEM((384,), F32),
            pltpu.VMEM((192,), F32),
            dma((CHUNKS,)),
            dma((2,)),
            dma((2,)),
            dma((CHUNKS,)),
            dma((CHUNKS,)),
            dma((CHUNKS, CHIPS)),
            dma((CHUNKS, CHIPS)),
            dma((CHIPS,)),
            dma((CHIPS,)),
            dma((CHUNKS, 2)),
            dma((CHUNKS, 2)),
            dma((CHUNKS,)),
            dma((3,)),
            dma((8,)),
        ],
        compiler_params=pltpu.CompilerParams(
            collective_id=0, has_side_effects=True, vmem_limit_bytes=62 * 1024 * 1024
        ),
        name="reduce",
    )(
        hidden_feats.T, mod_shift, mod_scale, head_w.T, head_b, latent_mean, latent_std,
        conv_in_w, conv_in_b, jnp.swapaxes(up_w, 2, 3), up_b,
    )
    decoded = pl.pallas_call(
        last_kernel,
        out_shape=pieces,
        in_specs=[hbm] * 4,
        out_specs=hbm,
        scratch_shapes=[
            pltpu.VMEM((6, 8, 2, 4, 8, 192), BF16),
            pltpu.VMEM((4, 64, 128), F32),
            pltpu.VMEM((3, 256, 768), BF16),
            pltpu.VMEM((2, 2, 2, 256, 768), BF16),
            *work,
            pltpu.VMEM((2, 8, 2, 4, 8, 192), BF16),
            dma((6,)),
        ],
        compiler_params=pltpu.CompilerParams(vmem_limit_bytes=62 * 1024 * 1024),
        name="last",
    )(done, state, first_w, second_w)
    return decoded.reshape(8, 64, 8, 192)


def solution(mesh):
    placed = (
        P("req", "sp"),
        P(("req", "sp")),
        P(("req", "sp")),
        P("sp", None),
        P(),
        P(),
        P(),
        P(),
        P(),
        P(),
        P(),
    )
    return jax.shard_map(
        shards, mesh=mesh, in_specs=placed, out_specs=P("req", None, "sp", None), check_vma=False
    )
```

```python
import jax
import jax.numpy as jnp
from jax import lax
from jax.experimental import pallas as pl
from jax.experimental.pallas import tpu as pltpu
from jax.sharding import PartitionSpec as P

F32 = jnp.float32
BF16 = jnp.bfloat16
MESH = pl.DeviceIdType.MESH

FEATS = 5120
LOCAL = 160
CHUNKS = 4
CHIPS = 16
GROUP = 32
FAR = 6
OFFSETS = [(dy, dz) for dz in (4, 3, 5, 2, 6, 1, 7) for dy in (1, 0)] + [(1, 0), (0, 0)]
SLOTS = (*range(1, FAR, 2), *range(FAR, CHIPS - 1))
NT = (((1,), (1,)), ((), ()))


def lanes(shape):
    return lax.broadcasted_iota(jnp.int32, shape, len(shape) - 1)


def rows(shape):
    return lax.broadcasted_iota(jnp.int32, shape, len(shape) - 2)


def square(width):
    return rows((width, width)) == lanes((width, width))


def to_column(row):
    return jnp.sum(jnp.where(square(row.shape[1]), row, 0.0), axis=1, keepdims=True)


def to_row(column):
    return jnp.sum(jnp.where(square(column.shape[0]), column, 0.0), axis=0, keepdims=True)


def tile16(row):
    wide = jnp.concatenate([row, jnp.zeros((1, 112), F32)], axis=1)
    for step in (16, 32, 64):
        wide = wide + pltpu.roll(wide, step, 1)
    return wide[:, 0:64]


def prepare_first(conv_w, first_w):
    for dx in range(3):
        for kt in range(3):
            for j in range(4):
                at = (kt * 4 + j) * 16
                for q in range(2):
                    inside = 0 <= j - q <= 2
                    tap = conv_w[kt, j - q, dx] if inside else jnp.zeros((16, 384), BF16)
                    first_w[dx, at : at + 16, q * 384 : (q + 1) * 384] = tap
        first_w[dx, 192:256, :] = jnp.zeros((64, 768), BF16)


def prepare_second(up_w, second_w):
    def split(first, middle, last):
        return {(0, 0): first, (0, 1): middle + last, (1, 0): first + middle, (1, 1): last}

    def part(i, carry):
        at = pl.ds(pl.multiple_of(i * 16, 16), 16)
        by_column = [split(*(up_w[dy, dx, at, :].astype(F32) for dy in range(3))) for dx in range(3)]
        for a in range(2):
            for alpha in range(2):
                combined = split(*(by_column[dx][a, alpha] for dx in range(3)))
                for b in range(2):
                    for beta in range(2):
                        second_w[a, b, beta, at, alpha * 384 : (alpha + 1) * 384] = combined[b, beta].astype(BF16)
        return carry

    lax.fori_loop(0, 12, part, 0)
    for a in range(2):
        for b in range(2):
            for beta in range(2):
                second_w[a, b, beta, 192:256, :] = jnp.zeros((64, 768), BF16)


def first_convolution(me, latent, previous, first_w, conv_b, taps, wide):
    lane = lanes((64, 128))
    parity, frame, half_row = lax.rem(lane // 16, 2), lax.rem(lane // 8, 2), lax.rem(lane, 8)
    above = jnp.where(parity == 1, pltpu.roll(latent, 16, 1), jnp.where(half_row == 0, 0.0, pltpu.roll(latent, 113, 1)))
    below = jnp.where(parity == 0, pltpu.roll(latent, 112, 1), jnp.where(half_row == 7, 0.0, pltpu.roll(latent, 15, 1)))
    for r in range(2):
        at = slice(r * 16, r * 16 + 16)
        low = slice(32 + r * 16, 48 + r * 16)
        now = jnp.concatenate([above[low], latent[at], latent[low], below[at]], axis=0)
        before = previous[r]
        last = jnp.where(frame == 1, pltpu.roll(now, 8, 1), pltpu.roll(before, 120, 1))
        previous[r] = now
        one = jnp.transpose(jnp.concatenate([before, last], axis=0))
        two = jnp.transpose(jnp.concatenate([now, jnp.zeros((64, 128), F32)], axis=0))
        for place, w in enumerate((1, 2, 0, 3)):
            u = 2 * w + r
            part = slice(place * 32, place * 32 + 32)
            taps[u * 32 : u * 32 + 32, 0:128] = one[part].astype(BF16)
            taps[u * 32 : u * 32 + 32, 128:256] = two[part].astype(BF16)

    inner = rows((2, 8, 384))
    whole = conv_b
    for dx in range(3):
        whole = whole + jnp.dot(taps[dx * 32 : dx * 32 + 192, :], first_w[dx], preferred_element_type=F32)
    for m in range(6):
        hidden = whole[m * 32 : m * 32 + 32]
        if m == 0:
            hidden = jnp.where(me == 0, 0.0, hidden)
        if m == 5:
            hidden = jnp.where(me == GROUP - 1, 0.0, hidden)
        upper, lower = hidden[:, 0:384], hidden[:, 384:768]
        over = jnp.where(inner == 0, 0.0, pltpu.roll(lower[16:32].reshape(2, 8, 384), 1, 1)).reshape(16, 384)
        under = jnp.where(inner == 7, 0.0, pltpu.roll(upper[0:16].reshape(2, 8, 384), 7, 1)).reshape(16, 384)
        at = slice(m * 32, m * 32 + 32)
        over = jnp.concatenate([over, lower[0:16]], axis=0).astype(BF16)
        under = jnp.concatenate([upper[16:32], under], axis=0).astype(BF16)
        upper, lower = upper.astype(BF16), lower.astype(BF16)
        for q, parts in enumerate(((over, upper, lower), (upper, lower, under))):
            for i, value in enumerate(parts):
                wide[q, at, i * 384 : (i + 1) * 384] = value


def second_convolution(second_w, up_b, wide, stage, ready, between=None):
    for a in range(2):
        if a == 1 and between is not None:
            between()
        for b in range(2):
            value = up_b
            for beta in range(2):
                left = wide[:, (b + beta) * 32 : (b + beta) * 32 + 128, a * 384 : a * 384 + 768].reshape(256, 768)
                value = value + lax.dot_general(left, second_w[a, b, beta], NT, preferred_element_type=F32)
            for q in range(2):
                for x in range(4):
                    at = (q * 4 + x) * 32
                    for half in range(2):
                        stage[half, pl.ds((q * 2 + a) * 256 + 2 * x + b, 32, stride=8), :] = value[
                            at : at + 32, half * 128 : (half + 1) * 128
                        ]
    for p in range(4):
        for parity in range(2):
            for f in range(2):
                at = pl.ds(p * 256 + parity * 128 + f * 64, 64)
                ready[f, :, parity, p, :, 0:128] = stage[0, at, :].reshape(8, 8, 128).astype(BF16)
                ready[f, :, parity, p, :, 128:192] = stage[1, at, :].reshape(8, 8, 128)[:, :, 0:64].astype(BF16)


def reduce_kernel(
    x_hbm, shift_hbm, scale_hbm, head_w_hbm, head_b_hbm, lat_mean_hbm, lat_std_hbm,
    conv_w_hbm, conv_b_hbm, up_w_hbm, up_b_hbm,
    out_hbm, state_hbm, first_hbm, second_hbm,
    x_buf, partial, sums, turned, own_stat, peer_stat, rest, give, got, across, crossed, parcel, arrived, stat_out, stat_in,
    sent, beside, conv_w, up_w, first_w, second_w, previous, taps, wide, stage, ready, state,
    shift_ref, scale_ref, head_w_ref, head_b_ref, lat_mean_ref, lat_std_ref, conv_b_ref, up_b_ref,
    x_sem, w_sem, stat_sem, core_send, core_recv, send_sem, recv_sem, ssend_sem, srecv_sem, hsend_sem, hrecv_sem,
    out_sem, keep_sem, small_sem, y_sem,
):
    me = lax.axis_index("sp")
    req = lax.axis_index("req")
    core = lax.rem(me, 2)
    chip = me // 2
    y, z = chip // 8, lax.rem(chip, 8)
    chips = [lax.rem(y + dy, 2) * 8 + lax.rem(z + dz, 8) for dy, dz in OFFSETS]
    partner = (req, chip * 2 + (1 - core))
    left, right = lax.rem(me + GROUP - 1, GROUP), lax.rem(me + 1, GROUP)
    other = jnp.where(core == 0, left, right)

    def remote(src, dst, send, recv, to):
        return pltpu.make_async_remote_copy(
            src_ref=src, dst_ref=dst, send_sem=send, recv_sem=recv, device_id=to, device_id_type=MESH
        )

    pairs = (
        (shift_hbm, shift_ref), (scale_hbm, scale_ref), (head_w_hbm, head_w_ref), (head_b_hbm, head_b_ref),
        (lat_mean_hbm, lat_mean_ref), (lat_std_hbm, lat_std_ref), (conv_b_hbm, conv_b_ref), (up_b_hbm, up_b_ref),
    )
    small = [pltpu.make_async_copy(src, dst, small_sem.at[i]) for i, (src, dst) in enumerate(pairs)]
    for copy in small:
        copy.start()
    x_copies = []
    for c in range(CHUNKS):
        copy = pltpu.make_async_copy(x_hbm.at[:, pl.ds(c * 2048, 2048)], x_buf.at[c], x_sem.at[c])
        copy.start()
        x_copies.append(copy)

    barrier = pltpu.get_barrier_semaphore()
    for to in chips[:-1]:
        pl.semaphore_signal(barrier, inc=1, device_id=(req, to * 2 + core), device_id_type=MESH)
    pl.semaphore_signal(barrier, inc=1, device_id=partner, device_id_type=MESH)
    pl.semaphore_signal(barrier, inc=1, device_id=(req, other), device_id_type=MESH)

    conv_copy = pltpu.make_async_copy(conv_w_hbm, conv_w, w_sem.at[0])
    up_copy = pltpu.make_async_copy(up_w_hbm, up_w, w_sem.at[1])
    conv_copy.start()
    up_copy.start()

    for copy in small:
        copy.wait()
    head = head_w_ref[...].astype(F32)
    folded = (1.0 + scale_ref[...].reshape(1, LOCAL)) * head
    weight_sum = jnp.sum(folded, axis=1, keepdims=True)
    shifted = jnp.sum(shift_ref[...].reshape(1, LOCAL) * head, axis=1, keepdims=True)
    centred = folded - weight_sum * (1.0 / LOCAL)
    high = centred.astype(BF16)
    low = (centred - high.astype(F32)).astype(BF16)
    weights = jnp.concatenate([high, low, jnp.ones((16, LOCAL), BF16)], axis=0)

    def core_copy(c):
        return remote(give.at[c], got.at[c], core_send.at[c], core_recv.at[c], partner)

    def gathered(c, to, core_to):
        at = (to * 2 + core_to) * 2
        return jnp.concatenate(
            [
                partial[c, pl.ds(parity * 64 + at + column, 8, stride=128), :]
                for column in range(2)
                for parity in range(2)
            ],
            axis=0,
        )

    def parcel_copy(c, k):
        return remote(
            parcel.at[c, k], arrived.at[c, k], send_sem.at[c, k], recv_sem.at[c, k], (req, chips[k] * 2 + core)
        )

    def merged(c, k):
        return gathered(c, chips[k], core) + got[c, k].astype(F32)

    def across_copy(c):
        return remote(
            across.at[c], crossed.at[c], y_sem.at[c, 0], y_sem.at[c, 1], (req, chips[CHIPS - 2] * 2 + core)
        )

    def dispatch_across(c):
        core_copy(c).wait_recv()
        for i in range(FAR // 2):
            across[c, i] = merged(c, 2 * i).astype(BF16)
        across_copy(c).start()

    def dispatch_near(c):
        for k in range(FAR, CHIPS - 1):
            parcel[c, k] = merged(c, k).astype(BF16)
            parcel_copy(c, k).start()
        rest[c] = merged(c, CHIPS - 1)

    def dispatch_far(c):
        across_copy(c).wait_recv()
        for i in range(FAR // 2):
            k = 2 * i + 1
            parcel[c, k] = (merged(c, k) + crossed[c, i].astype(F32)).astype(BF16)
            parcel_copy(c, k).start()

    for c in range(CHUNKS):
        x_copies[c].wait()

        def block(i, carry):
            products = []
            for f in range(2):
                x = x_buf[c, :, pl.ds(pl.multiple_of(f * 1024 + i * 256, 256), 256)]
                product = jnp.dot(weights, x, preferred_element_type=F32)
                products.append(product[0:64] + product[64:128])
                wide_x = x.astype(F32)
                power = jnp.sum(wide_x * wide_x, axis=0, keepdims=True)
                for half in range(2):
                    at = (c * 2 + f) * 8 + i * 2 + half
                    cut = slice(half * 128, half * 128 + 128)
                    sums[pl.ds(at, 1), :] = product[128:129, cut]
                    sums[pl.ds(64 + at, 1), :] = power[:, cut]
            for half in range(2):
                cut = slice(half * 128, half * 128 + 128)
                pair = jnp.concatenate([products[0][:, cut], products[1][:, cut]], axis=0)
                partial[c, pl.ds(pl.multiple_of((i * 2 + half) * 128, 128), 128), :] = jnp.transpose(pair)
            return carry

        lax.fori_loop(0, 4, block, 0, unroll=True)
    pl.semaphore_wait(barrier, 17)
    for c in range(CHUNKS):
        for k in range(CHIPS):
            give[c, k] = gathered(c, chips[k], 1 - core).astype(BF16)
        core_copy(c).start()

    turned[0:128, :] = jnp.transpose(sums[...])
    group = lax.rem(lanes((32, 128)) // 16, 4)
    quarters = [turned[pl.ds(parity * 64 + column, 32, stride=2), :] for column in range(2) for parity in range(2)]
    for c in range(CHUNKS):
        placed = [quarters[g] if g == c else pltpu.roll(quarters[g], (16 * (g - c)) % 128, 1) for g in range(4)]
        own_stat[c] = jnp.where(
            group == 0, placed[0], jnp.where(group == 1, placed[1], jnp.where(group == 2, placed[2], placed[3]))
        )
    own_row = jnp.concatenate([to_row(weight_sum), to_row(shifted)], axis=1)
    own_stat[4] = jnp.broadcast_to(own_row, (32, 128))
    stat_copy = remote(own_stat, peer_stat, stat_sem.at[0], stat_sem.at[1], partner)
    stat_copy.start()
    for c in range(CHUNKS):
        dispatch_across(c)
    dispatch_near(0)
    stat_copy.wait()

    low_half = lanes((32, 128)) < 64
    own = [own_stat[c] for c in range(5)]
    peer = [peer_stat[c] for c in range(5)]
    both = [own[c] + peer[c] for c in range(5)]
    turned_both = [pltpu.roll(both[c], 64, 1) for c in range(5)]
    lines = [jnp.where(low_half, own[c], pltpu.roll(peer[c], 64, 1)) for c in range(5)]
    lines = lines[0:4] + [
        jnp.where(low_half, turned_both[0], both[1]), jnp.where(low_half, turned_both[2], both[3]),
        lines[4], turned_both[4],
    ]
    for line in range(8):
        turned[pl.ds(line, 32, stride=8), :] = lines[line]

    def stat_remote(k):
        return remote(
            stat_out.at[k], stat_in.at[pl.ds(k * 8, 8)], ssend_sem.at[k], srecv_sem.at[k], (req, chips[k] * 2 + core)
        )

    for k in range(CHIPS):
        value = turned[pl.ds(pl.multiple_of((chips[k] * 2 + core) * 8, 8), 8), :]
        if k == CHIPS - 1:
            stat_in[k * 8 : k * 8 + 8, :] = value
        else:
            stat_out[k] = value
            stat_remote(k).start()

    dispatch_near(1)
    conv_copy.wait()
    prepare_first(conv_w, first_w)
    up_copy.wait()
    prepare_second(up_w, second_w)
    previous[...] = jnp.zeros((2, 64, 128), F32)
    keeps = [
        pltpu.make_async_copy(first_w, first_hbm, keep_sem.at[0]),
        pltpu.make_async_copy(second_w, second_hbm, keep_sem.at[1]),
    ]
    for copy in keeps:
        copy.start()

    dispatch_far(0)
    dispatch_near(2)
    dispatch_far(1)
    dispatch_far(2)
    for k in range(CHIPS - 1):
        stat_remote(k).wait_recv()
    total = jnp.sum(stat_in[...].reshape(CHIPS, 8, 128), axis=0)
    sums_of = [stat_in[pl.ds(c, CHIPS, stride=8), :] for c in range(4)]
    heads = stat_in[pl.ds(6, CHIPS, stride=8), :]
    heads = jnp.concatenate([heads, pltpu.roll(heads, 64, 1), jnp.zeros((96, 128), F32)], axis=0)
    heads = jnp.transpose(heads)[0:64, :]
    both_sums = total + pltpu.roll(total, 64, 1)
    means = both_sums[0:4] * (1.0 / FEATS)
    swapped = pltpu.roll(total, 64, 1)
    bias = to_column(total[7:8, 0:64] + head_b_ref[...].reshape(1, 64))
    std = to_column(tile16(lat_std_ref[...].reshape(1, 16)))
    shift = to_column(tile16(lat_mean_ref[...].reshape(1, 16)))
    centres, scales = [], []
    for c in range(CHUNKS):
        mean = means[c : c + 1]
        off = sums_of[c] * (1.0 / LOCAL) - mean
        off = jnp.concatenate([off, pltpu.roll(off, 64, 1), jnp.zeros((96, 128), F32)], axis=0)
        centres.append(jnp.dot(heads, off, precision=lax.Precision.HIGHEST, preferred_element_type=F32))
        power = (total if c % 2 == 0 else swapped)[4 + c // 2 : 5 + c // 2]
        scales.append(lax.rsqrt(power * (1.0 / FEATS) - mean * mean + 1e-06))

    lane = lanes((64, 128))
    conv_b = conv_b_ref[...].reshape(1, 384)
    conv_b = jnp.concatenate([conv_b, conv_b], axis=1)
    up_b = jnp.concatenate([up_b_ref[...].reshape(1, 192), jnp.zeros((1, 64), F32)], axis=1)

    def halo_copies(c):
        return [
            remote(sent.at[c], beside.at[c, side], hsend_sem.at[c, side], hrecv_sem.at[c, side], (req, to))
            for side, to in ((1, left), (0, right))
        ]

    def ends(c, action):
        to_left, to_right = halo_copies(c)
        pl.when(me > 0)(getattr(to_left, action))
        pl.when(me < GROUP - 1)(getattr(to_right, action))

    def finish(c):
        for k in SLOTS:
            parcel_copy(c, k).wait_recv()
        value = rest[c]
        for k in SLOTS:
            value = value + arrived[c, k].astype(F32)
        none = jnp.zeros((8, 128), F32)
        spread = []
        for g in range(4):
            spread += [value[g * 8 : g * 8 + 8], none]
        value = jnp.transpose(jnp.concatenate(spread + [jnp.zeros((64, 128), F32)], axis=0))
        value = jnp.where(lax.rem(lane // 8, 2) == 0, value[0:64], pltpu.roll(value[64:128], 8, 1))
        patches = (value + centres[c]) * scales[c] + bias
        sent[c] = (patches * std + shift).astype(BF16)
        ends(c, "start")

    def assembled(c):
        pl.when(me > 0)(halo_copies(c)[1].wait_recv)
        pl.when(me < GROUP - 1)(halo_copies(c)[0].wait_recv)
        own = sent[c].astype(F32)
        before = jnp.where(me == 0, 0.0, pltpu.roll(beside[c, 0].astype(F32), 32, 1))
        after = jnp.where(me == GROUP - 1, 0.0, pltpu.roll(beside[c, 1].astype(F32), 96, 1))
        return jnp.where(lane < 64, own, jnp.where(lane < 96, before, after))

    def out_copy(c):
        return pltpu.make_async_copy(ready.at[c], out_hbm.at[pl.ds(2 * c, 2)], out_sem.at[c])

    def decode(c):
        latent = assembled(c)
        first_convolution(me, latent, previous, first_w, conv_b, taps, wide)
        second_convolution(second_w, up_b, wide, stage, ready.at[c])
        out_copy(c).start()

    finish(0)
    dispatch_near(3)
    dispatch_far(3)
    finish(1)
    decode(0)
    finish(2)
    decode(1)
    finish(3)
    decode(2)

    state[2] = assembled(CHUNKS - 1)
    state[0:2] = previous[...]
    for i in range(6):
        state[3, i : i + 1, :] = conv_b[:, i * 128 : (i + 1) * 128]
    for i in range(2):
        state[3, 8 + i : 9 + i, :] = up_b[:, i * 128 : (i + 1) * 128]
    keeps.append(pltpu.make_async_copy(state, state_hbm, keep_sem.at[2]))
    keeps[2].start()
    for c in range(CHUNKS):
        if c < CHUNKS - 1:
            out_copy(c).wait()
        core_copy(c).wait_send()
        across_copy(c).wait_send()
        for k in SLOTS:
            parcel_copy(c, k).wait_send()
        ends(c, "wait_send")
    for k in range(CHIPS - 1):
        stat_remote(k).wait_send()
    for copy in keeps:
        copy.wait()


def last_kernel(
    done_hbm, state_hbm, first_hbm, second_hbm,
    out_hbm,
    done, state, first_w, second_w, previous, taps, wide, stage, ready, sem,
):
    me = lax.axis_index("sp")
    frames = 2 * (CHUNKS - 1)
    load_state = pltpu.make_async_copy(state_hbm, state, sem.at[0])
    load_first = pltpu.make_async_copy(first_hbm, first_w, sem.at[1])
    load_second = pltpu.make_async_copy(second_hbm, second_w, sem.at[2])
    load_done = pltpu.make_async_copy(done_hbm, done, sem.at[3])
    for copy in (load_state, load_first, load_second, load_done):
        copy.start()
    load_state.wait()
    previous[...] = state[0:2]
    conv_b = jnp.concatenate([state[3, i : i + 1, :] for i in range(6)], axis=1)
    up_b = jnp.concatenate([state[3, i : i + 1, :] for i in (8, 9)], axis=1)
    load_first.wait()
    first_convolution(me, state[2], previous, first_w, conv_b, taps, wide)
    load_second.wait()
    store_done = pltpu.make_async_copy(done, out_hbm.at[pl.ds(0, frames)], sem.at[4])

    def between():
        load_done.wait()
        store_done.start()

    second_convolution(second_w, up_b, wide, stage, ready, between)
    store = pltpu.make_async_copy(ready, out_hbm.at[pl.ds(frames, 2)], sem.at[5])
    store.start()
    store_done.wait()
    store.wait()


def shards(
    hidden_feats, mod_shift, mod_scale, head_w, head_b, latent_mean, latent_std, conv_in_w, conv_in_b, up_w, up_b
):
    hbm = pl.BlockSpec(memory_space=pltpu.HBM)
    dma = pltpu.SemaphoreType.DMA
    pieces = jax.ShapeDtypeStruct((8, 8, 2, 4, 8, 192), BF16)
    work = [
        pltpu.VMEM((2, 64, 128), F32),
        pltpu.VMEM((256, 256), BF16),
        pltpu.VMEM((2, 192, 1152), BF16),
        pltpu.VMEM((2, 1024, 128), F32),
    ]
    held = [
        jax.ShapeDtypeStruct((4, 64, 128), F32),
        jax.ShapeDtypeStruct((3, 256, 768), BF16),
        jax.ShapeDtypeStruct((2, 2, 2, 256, 768), BF16),
    ]
    done, state, first_w, second_w = pl.pallas_call(
        reduce_kernel,
        out_shape=[jax.ShapeDtypeStruct((6, 8, 2, 4, 8, 192), BF16)] + held,
        in_specs=[hbm] * 11,
        out_specs=[hbm] * 4,
        scratch_shapes=[
            pltpu.VMEM((CHUNKS, LOCAL, 2048), BF16),
            pltpu.VMEM((CHUNKS, 1024, 128), F32),
            pltpu.VMEM((128, 128), F32),
            pltpu.VMEM((256, 128), F32),
            pltpu.VMEM((5, 32, 128), F32),
            pltpu.VMEM((5, 32, 128), F32),
            pltpu.VMEM((CHUNKS, 32, 128), F32),
            pltpu.VMEM((CHUNKS, CHIPS, 32, 128), BF16),
            pltpu.VMEM((CHUNKS, CHIPS, 32, 128), BF16),
            pltpu.VMEM((CHUNKS, FAR // 2, 32, 128), BF16),
            pltpu.VMEM((CHUNKS, FAR // 2, 32, 128), BF16),
            pltpu.VMEM((CHUNKS, CHIPS, 32, 128), BF16),
            pltpu.VMEM((CHUNKS, CHIPS, 32, 128), BF16),
            pltpu.VMEM((CHIPS, 8, 128), F32),
            pltpu.VMEM((CHIPS * 8, 128), F32),
            pltpu.VMEM((CHUNKS, 64, 128), BF16),
            pltpu.VMEM((CHUNKS, 2, 64, 128), BF16),
            pltpu.VMEM((3, 3, 3, 16, 384), BF16),
            pltpu.VMEM((3, 3, 192, 384), BF16),
            pltpu.VMEM((3, 256, 768), BF16),
            pltpu.VMEM((2, 2, 2, 256, 768), BF16),
            *work,
            pltpu.VMEM((CHUNKS - 1, 2, 8, 2, 4, 8, 192), BF16),
            pltpu.VMEM((4, 64, 128), F32),
            pltpu.VMEM((LOCAL,), F32),
            pltpu.VMEM((LOCAL,), F32),
            pltpu.VMEM((64, LOCAL), BF16),
            pltpu.VMEM((64,), F32),
            pltpu.VMEM((16,), F32),
            pltpu.VMEM((16,), F32),
            pltpu.VMEM((384,), F32),
            pltpu.VMEM((192,), F32),
            dma((CHUNKS,)),
            dma((2,)),
            dma((2,)),
            dma((CHUNKS,)),
            dma((CHUNKS,)),
            dma((CHUNKS, CHIPS)),
            dma((CHUNKS, CHIPS)),
            dma((CHIPS,)),
            dma((CHIPS,)),
            dma((CHUNKS, 2)),
            dma((CHUNKS, 2)),
            dma((CHUNKS,)),
            dma((3,)),
            dma((8,)),
            dma((CHUNKS, 2)),
        ],
        compiler_params=pltpu.CompilerParams(
            collective_id=0, has_side_effects=True, vmem_limit_bytes=62 * 1024 * 1024
        ),
        name="reduce",
    )(
        hidden_feats.T, mod_shift, mod_scale, head_w.T, head_b, latent_mean, latent_std,
        conv_in_w, conv_in_b, jnp.swapaxes(up_w, 2, 3), up_b,
    )
    decoded = pl.pallas_call(
        last_kernel,
        out_shape=pieces,
        in_specs=[hbm] * 4,
        out_specs=hbm,
        scratch_shapes=[
            pltpu.VMEM((6, 8, 2, 4, 8, 192), BF16),
            pltpu.VMEM((4, 64, 128), F32),
            pltpu.VMEM((3, 256, 768), BF16),
            pltpu.VMEM((2, 2, 2, 256, 768), BF16),
            *work,
            pltpu.VMEM((2, 8, 2, 4, 8, 192), BF16),
            dma((6,)),
        ],
        compiler_params=pltpu.CompilerParams(vmem_limit_bytes=62 * 1024 * 1024),
        name="last",
    )(done, state, first_w, second_w)
    return decoded.reshape(8, 64, 8, 192)


def solution(mesh):
    placed = (
        P("req", "sp"),
        P(("req", "sp")),
        P(("req", "sp")),
        P("sp", None),
        P(),
        P(),
        P(),
        P(),
        P(),
        P(),
        P(),
    )
    return jax.shard_map(
        shards, mesh=mesh, in_specs=placed, out_specs=P("req", None, "sp", None), check_vma=False
    )
```

```python
import jax
import jax.numpy as jnp
from jax import lax
from jax.experimental import pallas as pl
from jax.experimental.pallas import tpu as pltpu
from jax.sharding import PartitionSpec as P

F32 = jnp.float32
BF16 = jnp.bfloat16
MESH = pl.DeviceIdType.MESH

FEATS = 5120
LOCAL = 160
CHUNKS = 4
CHIPS = 16
GROUP = 32
FAR = 6
OFFSETS = [(dy, dz) for dz in (4, 3, 5, 2, 6, 1, 7) for dy in (1, 0)] + [(1, 0), (0, 0)]
SLOTS = (*range(1, FAR, 2), *range(FAR, CHIPS - 1))
NT = (((1,), (1,)), ((), ()))


def lanes(shape):
    return lax.broadcasted_iota(jnp.int32, shape, len(shape) - 1)


def rows(shape):
    return lax.broadcasted_iota(jnp.int32, shape, len(shape) - 2)


def square(width):
    return rows((width, width)) == lanes((width, width))


def to_column(row):
    return jnp.sum(jnp.where(square(row.shape[1]), row, 0.0), axis=1, keepdims=True)


def to_row(column):
    return jnp.sum(jnp.where(square(column.shape[0]), column, 0.0), axis=0, keepdims=True)


def tile16(row):
    wide = jnp.concatenate([row, jnp.zeros((1, 112), F32)], axis=1)
    for step in (16, 32, 64):
        wide = wide + pltpu.roll(wide, step, 1)
    return wide[:, 0:64]


def prepare_first(conv_w, first_w):
    for dx in range(3):
        for kt in range(3):
            for j in range(4):
                at = (kt * 4 + j) * 16
                for q in range(2):
                    inside = 0 <= j - q <= 2
                    tap = conv_w[kt, j - q, dx] if inside else jnp.zeros((16, 384), BF16)
                    first_w[dx, at : at + 16, q * 384 : (q + 1) * 384] = tap
        first_w[dx, 192:256, :] = jnp.zeros((64, 768), BF16)


def prepare_second(up_w, second_w):
    def split(first, middle, last):
        return {(0, 0): first, (0, 1): middle + last, (1, 0): first + middle, (1, 1): last}

    def part(i, carry):
        at = pl.ds(pl.multiple_of(i * 16, 16), 16)
        by_column = [split(*(up_w[dy, dx, at, :].astype(F32) for dy in range(3))) for dx in range(3)]
        for a in range(2):
            for alpha in range(2):
                combined = split(*(by_column[dx][a, alpha] for dx in range(3)))
                for b in range(2):
                    for beta in range(2):
                        second_w[a, b, beta, at, alpha * 384 : (alpha + 1) * 384] = combined[b, beta].astype(BF16)
        return carry

    lax.fori_loop(0, 12, part, 0)
    for a in range(2):
        for b in range(2):
            for beta in range(2):
                second_w[a, b, beta, 192:256, :] = jnp.zeros((64, 768), BF16)


def first_convolution(me, latent, previous, first_w, conv_b, taps, wide):
    lane = lanes((64, 128))
    parity, frame, half_row = lax.rem(lane // 16, 2), lax.rem(lane // 8, 2), lax.rem(lane, 8)
    above = jnp.where(parity == 1, pltpu.roll(latent, 16, 1), jnp.where(half_row == 0, 0.0, pltpu.roll(latent, 113, 1)))
    below = jnp.where(parity == 0, pltpu.roll(latent, 112, 1), jnp.where(half_row == 7, 0.0, pltpu.roll(latent, 15, 1)))
    for r in range(2):
        at = slice(r * 16, r * 16 + 16)
        low = slice(32 + r * 16, 48 + r * 16)
        now = jnp.concatenate([above[low], latent[at], latent[low], below[at]], axis=0)
        before = previous[r]
        last = jnp.where(frame == 1, pltpu.roll(now, 8, 1), pltpu.roll(before, 120, 1))
        previous[r] = now
        one = jnp.transpose(jnp.concatenate([before, last], axis=0))
        two = jnp.transpose(jnp.concatenate([now, jnp.zeros((64, 128), F32)], axis=0))
        for place, w in enumerate((1, 2, 0, 3)):
            u = 2 * w + r
            part = slice(place * 32, place * 32 + 32)
            taps[u * 32 : u * 32 + 32, 0:128] = one[part].astype(BF16)
            taps[u * 32 : u * 32 + 32, 128:256] = two[part].astype(BF16)

    inner = rows((2, 8, 384))
    whole = conv_b
    for dx in range(3):
        whole = whole + jnp.dot(taps[dx * 32 : dx * 32 + 192, :], first_w[dx], preferred_element_type=F32)
    for m in range(6):
        hidden = whole[m * 32 : m * 32 + 32]
        if m == 0:
            hidden = jnp.where(me == 0, 0.0, hidden)
        if m == 5:
            hidden = jnp.where(me == GROUP - 1, 0.0, hidden)
        upper, lower = hidden[:, 0:384], hidden[:, 384:768]
        over = jnp.where(inner == 0, 0.0, pltpu.roll(lower[16:32].reshape(2, 8, 384), 1, 1)).reshape(16, 384)
        under = jnp.where(inner == 7, 0.0, pltpu.roll(upper[0:16].reshape(2, 8, 384), 7, 1)).reshape(16, 384)
        at = slice(m * 32, m * 32 + 32)
        over = jnp.concatenate([over, lower[0:16]], axis=0).astype(BF16)
        under = jnp.concatenate([upper[16:32], under], axis=0).astype(BF16)
        upper, lower = upper.astype(BF16), lower.astype(BF16)
        for q, parts in enumerate(((over, upper, lower), (upper, lower, under))):
            for i, value in enumerate(parts):
                wide[q, at, i * 384 : (i + 1) * 384] = value


def second_convolution(second_w, up_b, wide, stage, ready, between=None):
    for a in range(2):
        if a == 1 and between is not None:
            between()
        for b in range(2):
            value = up_b
            for beta in range(2):
                left = wide[:, (b + beta) * 32 : (b + beta) * 32 + 128, a * 384 : a * 384 + 768].reshape(256, 768)
                value = value + lax.dot_general(left, second_w[a, b, beta], NT, preferred_element_type=F32)
            for q in range(2):
                for x in range(4):
                    at = (q * 4 + x) * 32
                    for half in range(2):
                        stage[half, pl.ds((q * 2 + a) * 256 + 2 * x + b, 32, stride=8), :] = value[
                            at : at + 32, half * 128 : (half + 1) * 128
                        ]
    for p in range(4):
        for parity in range(2):
            for f in range(2):
                at = pl.ds(p * 256 + parity * 128 + f * 64, 64)
                ready[f, :, parity, p, :, 0:128] = stage[0, at, :].reshape(8, 8, 128).astype(BF16)
                ready[f, :, parity, p, :, 128:192] = stage[1, at, :].reshape(8, 8, 128)[:, :, 0:64].astype(BF16)


def reduce_kernel(
    x_hbm, shift_hbm, scale_hbm, head_w_hbm, head_b_hbm, lat_mean_hbm, lat_std_hbm,
    conv_w_hbm, conv_b_hbm, up_w_hbm, up_b_hbm,
    out_hbm, state_hbm, first_hbm, second_hbm,
    x_buf, partial, sums, turned, own_stat, peer_stat, rest, give, got, across, crossed, parcel, arrived, stat_out, stat_in,
    sent, beside, conv_w, up_w, first_w, second_w, previous, taps, wide, stage, ready, state,
    shift_ref, scale_ref, head_w_ref, head_b_ref, lat_mean_ref, lat_std_ref, conv_b_ref, up_b_ref,
    x_sem, w_sem, stat_sem, core_send, core_recv, send_sem, recv_sem, ssend_sem, srecv_sem, hsend_sem, hrecv_sem,
    out_sem, keep_sem, small_sem, y_sem,
):
    me = lax.axis_index("sp")
    req = lax.axis_index("req")
    core = lax.rem(me, 2)
    chip = me // 2
    y, z = chip // 8, lax.rem(chip, 8)
    chips = [lax.rem(y + dy, 2) * 8 + lax.rem(z + dz, 8) for dy, dz in OFFSETS]
    partner = (req, chip * 2 + (1 - core))
    left, right = lax.rem(me + GROUP - 1, GROUP), lax.rem(me + 1, GROUP)
    other = jnp.where(core == 0, left, right)

    def remote(src, dst, send, recv, to):
        return pltpu.make_async_remote_copy(
            src_ref=src, dst_ref=dst, send_sem=send, recv_sem=recv, device_id=to, device_id_type=MESH
        )

    pairs = (
        (shift_hbm, shift_ref), (scale_hbm, scale_ref), (head_w_hbm, head_w_ref), (head_b_hbm, head_b_ref),
        (lat_mean_hbm, lat_mean_ref), (lat_std_hbm, lat_std_ref), (conv_b_hbm, conv_b_ref), (up_b_hbm, up_b_ref),
    )
    small = [pltpu.make_async_copy(src, dst, small_sem.at[i]) for i, (src, dst) in enumerate(pairs)]
    for copy in small:
        copy.start()
    x_copies = []
    for c in range(CHUNKS):
        copy = pltpu.make_async_copy(x_hbm.at[:, pl.ds(c * 2048, 2048)], x_buf.at[c], x_sem.at[c])
        copy.start()
        x_copies.append(copy)

    barrier = pltpu.get_barrier_semaphore()
    for to in chips[:-1]:
        pl.semaphore_signal(barrier, inc=1, device_id=(req, to * 2 + core), device_id_type=MESH)
    pl.semaphore_signal(barrier, inc=1, device_id=partner, device_id_type=MESH)
    pl.semaphore_signal(barrier, inc=1, device_id=(req, other), device_id_type=MESH)

    conv_copy = pltpu.make_async_copy(conv_w_hbm, conv_w, w_sem.at[0])
    up_copy = pltpu.make_async_copy(up_w_hbm, up_w, w_sem.at[1])
    conv_copy.start()
    up_copy.start()

    for copy in small:
        copy.wait()
    head = head_w_ref[...].astype(F32)
    folded = (1.0 + scale_ref[...].reshape(1, LOCAL)) * head
    weight_sum = jnp.sum(folded, axis=1, keepdims=True)
    shifted = jnp.sum(shift_ref[...].reshape(1, LOCAL) * head, axis=1, keepdims=True)
    centred = folded - weight_sum * (1.0 / LOCAL)
    high = centred.astype(BF16)
    low = (centred - high.astype(F32)).astype(BF16)
    weights = jnp.concatenate([high, low, jnp.ones((16, LOCAL), BF16)], axis=0)

    def core_copy(c):
        return remote(give.at[c], got.at[c], core_send.at[c], core_recv.at[c], partner)

    def gathered(c, to, core_to):
        at = (to * 2 + core_to) * 2
        return jnp.concatenate(
            [
                partial[c, pl.ds(parity * 64 + at + column, 8, stride=128), :]
                for column in range(2)
                for parity in range(2)
            ],
            axis=0,
        )

    def parcel_copy(c, k):
        return remote(
            parcel.at[c, k], arrived.at[c, k], send_sem.at[c, k], recv_sem.at[c, k], (req, chips[k] * 2 + core)
        )

    def merged(c, k):
        return gathered(c, chips[k], core) + got[c, k].astype(F32)

    def across_copy(c):
        return remote(
            across.at[c], crossed.at[c], y_sem.at[c, 0], y_sem.at[c, 1], (req, chips[CHIPS - 2] * 2 + core)
        )

    def dispatch_across(c):
        core_copy(c).wait_recv()
        for i in range(FAR // 2):
            across[c, i] = merged(c, 2 * i).astype(BF16)
        across_copy(c).start()

    def dispatch_near(c):
        for k in range(FAR, CHIPS - 1):
            parcel[c, k] = merged(c, k).astype(BF16)
            parcel_copy(c, k).start()
        rest[c] = merged(c, CHIPS - 1)

    def dispatch_far(c):
        across_copy(c).wait_recv()
        for i in range(FAR // 2):
            k = 2 * i + 1
            parcel[c, k] = (merged(c, k) + crossed[c, i].astype(F32)).astype(BF16)
            parcel_copy(c, k).start()

    for c in range(CHUNKS):
        x_copies[c].wait()

        def block(i, carry):
            products = []
            for f in range(2):
                x = x_buf[c, :, pl.ds(pl.multiple_of(f * 1024 + i * 256, 256), 256)]
                product = jnp.dot(weights, x, preferred_element_type=F32)
                products.append(product[0:64] + product[64:128])
                wide_x = x.astype(F32)
                power = jnp.sum(wide_x * wide_x, axis=0, keepdims=True)
                for half in range(2):
                    at = (c * 2 + f) * 8 + i * 2 + half
                    cut = slice(half * 128, half * 128 + 128)
                    sums[pl.ds(at, 1), :] = product[128:129, cut]
                    sums[pl.ds(64 + at, 1), :] = power[:, cut]
            for half in range(2):
                cut = slice(half * 128, half * 128 + 128)
                pair = jnp.concatenate([products[0][:, cut], products[1][:, cut]], axis=0)
                partial[c, pl.ds(pl.multiple_of((i * 2 + half) * 128, 128), 128), :] = jnp.transpose(pair)
            return carry

        lax.fori_loop(0, 4, block, 0, unroll=True)
    pl.semaphore_wait(barrier, 17)
    for c in range(CHUNKS):
        for k in range(CHIPS):
            give[c, k] = gathered(c, chips[k], 1 - core).astype(BF16)
        core_copy(c).start()

    turned[0:128, :] = jnp.transpose(sums[...])
    group = lax.rem(lanes((32, 128)) // 16, 4)
    quarters = [turned[pl.ds(parity * 64 + column, 32, stride=2), :] for column in range(2) for parity in range(2)]
    for c in range(CHUNKS):
        placed = [quarters[g] if g == c else pltpu.roll(quarters[g], (16 * (g - c)) % 128, 1) for g in range(4)]
        own_stat[c] = jnp.where(
            group == 0, placed[0], jnp.where(group == 1, placed[1], jnp.where(group == 2, placed[2], placed[3]))
        )
    own_row = jnp.concatenate([to_row(weight_sum), to_row(shifted)], axis=1)
    own_stat[4] = jnp.broadcast_to(own_row, (32, 128))
    stat_copy = remote(own_stat, peer_stat, stat_sem.at[0], stat_sem.at[1], partner)
    stat_copy.start()
    for c in range(CHUNKS):
        dispatch_across(c)
    dispatch_near(0)
    stat_copy.wait()

    low_half = lanes((32, 128)) < 64
    own = [own_stat[c] for c in range(5)]
    peer = [peer_stat[c] for c in range(5)]
    both = [own[c] + peer[c] for c in range(5)]
    turned_both = [pltpu.roll(both[c], 64, 1) for c in range(5)]
    lines = [jnp.where(low_half, own[c], pltpu.roll(peer[c], 64, 1)) for c in range(5)]
    lines = lines[0:4] + [
        jnp.where(low_half, turned_both[0], both[1]), jnp.where(low_half, turned_both[2], both[3]),
        lines[4], turned_both[4],
    ]
    for line in range(8):
        turned[pl.ds(line, 32, stride=8), :] = lines[line]

    def stat_remote(k):
        return remote(
            stat_out.at[k], stat_in.at[pl.ds(k * 8, 8)], ssend_sem.at[k], srecv_sem.at[k], (req, chips[k] * 2 + core)
        )

    for k in range(CHIPS):
        value = turned[pl.ds(pl.multiple_of((chips[k] * 2 + core) * 8, 8), 8), :]
        if k == CHIPS - 1:
            stat_in[k * 8 : k * 8 + 8, :] = value
        else:
            stat_out[k] = value
            stat_remote(k).start()

    dispatch_near(1)
    conv_copy.wait()
    prepare_first(conv_w, first_w)
    up_copy.wait()
    prepare_second(up_w, second_w)
    previous[...] = jnp.zeros((2, 64, 128), F32)
    keeps = [
        pltpu.make_async_copy(first_w, first_hbm, keep_sem.at[0]),
        pltpu.make_async_copy(second_w, second_hbm, keep_sem.at[1]),
    ]
    for copy in keeps:
        copy.start()

    dispatch_far(0)
    dispatch_near(2)
    dispatch_far(1)
    dispatch_far(2)
    for k in range(CHIPS - 1):
        stat_remote(k).wait_recv()
    total = jnp.sum(stat_in[0 : CHIPS * 8, :].reshape(CHIPS, 8, 128), axis=0)
    sums_of = [stat_in[pl.ds(c, CHIPS, stride=8), :] for c in range(4)]
    heads = stat_in[pl.ds(6, CHIPS, stride=8), :]
    heads = jnp.concatenate([heads, pltpu.roll(heads, 64, 1), jnp.zeros((96, 128), F32)], axis=0)
    heads = jnp.transpose(heads)[0:64, :]
    both_sums = total + pltpu.roll(total, 64, 1)
    means = both_sums[0:4] * (1.0 / FEATS)
    swapped = pltpu.roll(total, 64, 1)
    bias = to_column(total[7:8, 0:64] + head_b_ref[...].reshape(1, 64))
    std = to_column(tile16(lat_std_ref[...].reshape(1, 16)))
    shift = to_column(tile16(lat_mean_ref[...].reshape(1, 16)))
    centres, scales = [], []
    for c in range(CHUNKS):
        mean = means[c : c + 1]
        off = sums_of[c] * (1.0 / LOCAL) - mean
        off = jnp.concatenate([off, pltpu.roll(off, 64, 1), jnp.zeros((96, 128), F32)], axis=0)
        centres.append(jnp.dot(heads, off, precision=lax.Precision.HIGHEST, preferred_element_type=F32))
        power = (total if c % 2 == 0 else swapped)[4 + c // 2 : 5 + c // 2]
        scales.append(lax.rsqrt(power * (1.0 / FEATS) - mean * mean + 1e-06))

    lane = lanes((64, 128))
    conv_b = conv_b_ref[...].reshape(1, 384)
    conv_b = jnp.concatenate([conv_b, conv_b], axis=1)
    up_b = jnp.concatenate([up_b_ref[...].reshape(1, 192), jnp.zeros((1, 64), F32)], axis=1)

    def halo_copies(c):
        return [
            remote(sent.at[c], beside.at[c, side], hsend_sem.at[c, side], hrecv_sem.at[c, side], (req, to))
            for side, to in ((1, left), (0, right))
        ]

    def ends(c, action):
        to_left, to_right = halo_copies(c)
        pl.when(me > 0)(getattr(to_left, action))
        pl.when(me < GROUP - 1)(getattr(to_right, action))

    def finish(c):
        for k in SLOTS:
            parcel_copy(c, k).wait_recv()
        value = rest[c]
        for k in SLOTS:
            value = value + arrived[c, k].astype(F32)
        none = jnp.zeros((8, 128), F32)
        spread = []
        for g in range(4):
            spread += [value[g * 8 : g * 8 + 8], none]
        value = jnp.transpose(jnp.concatenate(spread + [jnp.zeros((64, 128), F32)], axis=0))
        value = jnp.where(lax.rem(lane // 8, 2) == 0, value[0:64], pltpu.roll(value[64:128], 8, 1))
        patches = (value + centres[c]) * scales[c] + bias
        sent[c] = (patches * std + shift).astype(BF16)
        ends(c, "start")

    def assembled(c):
        pl.when(me > 0)(halo_copies(c)[1].wait_recv)
        pl.when(me < GROUP - 1)(halo_copies(c)[0].wait_recv)
        own = sent[c].astype(F32)
        before = jnp.where(me == 0, 0.0, pltpu.roll(beside[c, 0].astype(F32), 32, 1))
        after = jnp.where(me == GROUP - 1, 0.0, pltpu.roll(beside[c, 1].astype(F32), 96, 1))
        return jnp.where(lane < 64, own, jnp.where(lane < 96, before, after))

    def out_copy(c):
        return pltpu.make_async_copy(ready.at[c], out_hbm.at[pl.ds(2 * c, 2)], out_sem.at[c])

    def decode(c):
        latent = assembled(c)
        first_convolution(me, latent, previous, first_w, conv_b, taps, wide)
        second_convolution(second_w, up_b, wide, stage, ready.at[c])
        out_copy(c).start()

    finish(0)
    dispatch_near(3)
    dispatch_far(3)
    finish(1)
    decode(0)
    finish(2)
    decode(1)
    finish(3)
    decode(2)

    state[2] = assembled(CHUNKS - 1)
    state[0:2] = previous[...]
    for i in range(6):
        state[3, i : i + 1, :] = conv_b[:, i * 128 : (i + 1) * 128]
    for i in range(2):
        state[3, 8 + i : 9 + i, :] = up_b[:, i * 128 : (i + 1) * 128]
    keeps.append(pltpu.make_async_copy(state, state_hbm, keep_sem.at[2]))
    keeps[2].start()
    for c in range(CHUNKS):
        if c < CHUNKS - 1:
            out_copy(c).wait()
        core_copy(c).wait_send()
        across_copy(c).wait_send()
        for k in SLOTS:
            parcel_copy(c, k).wait_send()
        ends(c, "wait_send")
    for k in range(CHIPS - 1):
        stat_remote(k).wait_send()
    for copy in keeps:
        copy.wait()


def last_kernel(
    done_hbm, state_hbm, first_hbm, second_hbm,
    out_hbm,
    done, state, first_w, second_w, previous, taps, wide, stage, ready, sem,
):
    me = lax.axis_index("sp")
    frames = 2 * (CHUNKS - 1)
    load_state = pltpu.make_async_copy(state_hbm, state, sem.at[0])
    load_first = pltpu.make_async_copy(first_hbm, first_w, sem.at[1])
    load_second = pltpu.make_async_copy(second_hbm, second_w, sem.at[2])
    load_done = pltpu.make_async_copy(done_hbm, done, sem.at[3])
    for copy in (load_state, load_first, load_second, load_done):
        copy.start()
    load_state.wait()
    previous[...] = state[0:2]
    conv_b = jnp.concatenate([state[3, i : i + 1, :] for i in range(6)], axis=1)
    up_b = jnp.concatenate([state[3, i : i + 1, :] for i in (8, 9)], axis=1)
    load_first.wait()
    first_convolution(me, state[2], previous, first_w, conv_b, taps, wide)
    load_second.wait()
    store_done = pltpu.make_async_copy(done, out_hbm.at[pl.ds(0, frames)], sem.at[4])

    def between():
        load_done.wait()
        store_done.start()

    second_convolution(second_w, up_b, wide, stage, ready, between)
    store = pltpu.make_async_copy(ready, out_hbm.at[pl.ds(frames, 2)], sem.at[5])
    store.start()
    store_done.wait()
    store.wait()


def shards(
    hidden_feats, mod_shift, mod_scale, head_w, head_b, latent_mean, latent_std, conv_in_w, conv_in_b, up_w, up_b
):
    hbm = pl.BlockSpec(memory_space=pltpu.HBM)
    dma = pltpu.SemaphoreType.DMA
    pieces = jax.ShapeDtypeStruct((8, 8, 2, 4, 8, 192), BF16)
    work = [
        pltpu.VMEM((2, 64, 128), F32),
        pltpu.VMEM((256, 256), BF16),
        pltpu.VMEM((2, 192, 1152), BF16),
        pltpu.VMEM((2, 1032, 128), F32),
    ]
    held = [
        jax.ShapeDtypeStruct((4, 64, 128), F32),
        jax.ShapeDtypeStruct((3, 256, 768), BF16),
        jax.ShapeDtypeStruct((2, 2, 2, 256, 768), BF16),
    ]
    done, state, first_w, second_w = pl.pallas_call(
        reduce_kernel,
        out_shape=[jax.ShapeDtypeStruct((6, 8, 2, 4, 8, 192), BF16)] + held,
        in_specs=[hbm] * 11,
        out_specs=[hbm] * 4,
        scratch_shapes=[
            pltpu.VMEM((CHUNKS, LOCAL, 2048), BF16),
            pltpu.VMEM((CHUNKS, 1152, 128), F32),
            pltpu.VMEM((128, 128), F32),
            pltpu.VMEM((264, 128), F32),
            pltpu.VMEM((5, 32, 128), F32),
            pltpu.VMEM((5, 32, 128), F32),
            pltpu.VMEM((CHUNKS, 32, 128), F32),
            pltpu.VMEM((CHUNKS, CHIPS, 32, 128), BF16),
            pltpu.VMEM((CHUNKS, CHIPS, 32, 128), BF16),
            pltpu.VMEM((CHUNKS, FAR // 2, 32, 128), BF16),
            pltpu.VMEM((CHUNKS, FAR // 2, 32, 128), BF16),
            pltpu.VMEM((CHUNKS, CHIPS, 32, 128), BF16),
            pltpu.VMEM((CHUNKS, CHIPS, 32, 128), BF16),
            pltpu.VMEM((CHIPS, 8, 128), F32),
            pltpu.VMEM((CHIPS * 8 + 8, 128), F32),
            pltpu.VMEM((CHUNKS, 64, 128), BF16),
            pltpu.VMEM((CHUNKS, 2, 64, 128), BF16),
            pltpu.VMEM((3, 3, 3, 16, 384), BF16),
            pltpu.VMEM((3, 3, 192, 384), BF16),
            pltpu.VMEM((3, 256, 768), BF16),
            pltpu.VMEM((2, 2, 2, 256, 768), BF16),
            *work,
            pltpu.VMEM((CHUNKS - 1, 2, 8, 2, 4, 8, 192), BF16),
            pltpu.VMEM((4, 64, 128), F32),
            pltpu.VMEM((LOCAL,), F32),
            pltpu.VMEM((LOCAL,), F32),
            pltpu.VMEM((64, LOCAL), BF16),
            pltpu.VMEM((64,), F32),
            pltpu.VMEM((16,), F32),
            pltpu.VMEM((16,), F32),
            pltpu.VMEM((384,), F32),
            pltpu.VMEM((192,), F32),
            dma((CHUNKS,)),
            dma((2,)),
            dma((2,)),
            dma((CHUNKS,)),
            dma((CHUNKS,)),
            dma((CHUNKS, CHIPS)),
            dma((CHUNKS, CHIPS)),
            dma((CHIPS,)),
            dma((CHIPS,)),
            dma((CHUNKS, 2)),
            dma((CHUNKS, 2)),
            dma((CHUNKS,)),
            dma((3,)),
            dma((8,)),
            dma((CHUNKS, 2)),
        ],
        compiler_params=pltpu.CompilerParams(
            collective_id=0, has_side_effects=True, vmem_limit_bytes=62 * 1024 * 1024
        ),
        name="reduce",
    )(
        hidden_feats.T, mod_shift, mod_scale, head_w.T, head_b, latent_mean, latent_std,
        conv_in_w, conv_in_b, jnp.swapaxes(up_w, 2, 3), up_b,
    )
    decoded = pl.pallas_call(
        last_kernel,
        out_shape=pieces,
        in_specs=[hbm] * 4,
        out_specs=hbm,
        scratch_shapes=[
            pltpu.VMEM((6, 8, 2, 4, 8, 192), BF16),
            pltpu.VMEM((4, 64, 128), F32),
            pltpu.VMEM((3, 256, 768), BF16),
            pltpu.VMEM((2, 2, 2, 256, 768), BF16),
            *work,
            pltpu.VMEM((2, 8, 2, 4, 8, 192), BF16),
            dma((6,)),
        ],
        compiler_params=pltpu.CompilerParams(vmem_limit_bytes=62 * 1024 * 1024),
        name="last",
    )(done, state, first_w, second_w)
    return decoded.reshape(8, 64, 8, 192)


def solution(mesh):
    placed = (
        P("req", "sp"),
        P(("req", "sp")),
        P(("req", "sp")),
        P("sp", None),
        P(),
        P(),
        P(),
        P(),
        P(),
        P(),
        P(),
    )
    return jax.shard_map(
        shards, mesh=mesh, in_specs=placed, out_specs=P("req", None, "sp", None), check_vma=False
    )
```
